32 devices in a mesh: blk: 16 (over z, x, core), col: 2 (over y).
Axes of the slice: x: 2, y: 2, z: 4, core: 2. Of those that a mesh axis runs over, the one named last changes fastest.
Arguments:
- feat1: bfloat16 [64, 96, 256], P('blk', 'col'), may hold values from -40 to 40
- feat2: bfloat16 [64, 96, 256], P('blk', 'col'), may hold values from -40 to 40
Outputs:
- flow: float32 [2, 64, 96], P(None, 'blk', 'col')
- grad_flow: float32 [2, 64, 96], P(None, 'blk', 'col')
- grad_warped: float32 [64, 96, 256], P('blk', 'col')
The draws below stay inside these ranges and needn't reach their ends.
All inputs are finite; a program needn't handle non-finite values.
Results may differ from the reference program's by a relative error of at most 0.0075.
Values may be sent and summed in bfloat16 or wider, within the bound.
A program may use at most 64 MiB of HBM per device.

```python
import math
import jax
import jax.numpy as jnp
from jax import lax

C = 256
H = 64
W = 96


def make_pair(key):
    count = H * W
    base_two = jnp.clip(jax.random.normal(jax.random.fold_in(key, 11), (count, C), jnp.float32), -5.0, 5.0)
    base_one = jnp.clip(jax.random.normal(jax.random.fold_in(key, 12), (count, C), jnp.float32), -5.0, 5.0)
    target = base_two
    source = base_one
    return (source.reshape(H, W, C), target.reshape(H, W, C))


def draw_feat1(key, part):
    return make_pair(key)[0].astype(jnp.bfloat16)


def draw_feat2(key, part):
    return make_pair(key)[1].astype(jnp.bfloat16)


def setup_inputs(seed: int = 0) -> dict:
    streams_of = jax.random.split(jax.random.key(seed), 3)
    feat1 = draw_feat1(jax.random.fold_in(streams_of[2], 71), 0)
    feat2 = draw_feat2(jax.random.fold_in(streams_of[2], 71), 0)
    return dict(feat1=feat1, feat2=feat2)


ssim_one = 0.01
ssim_two = 0.03
charb_sq = 0.0001

def box_valid(padded):
    rows_out = padded.shape[0] - 2
    cols_out = padded.shape[1] - 2
    total = jnp.zeros((rows_out, cols_out) + padded.shape[2:], padded.dtype)
    for offset_r in range(3):
        for offset_c in range(3):
            total = total + padded[offset_r:offset_r + rows_out, offset_c:offset_c + cols_out]
    return total / 9.0

def box_zero(values):
    return box_valid(jnp.pad(values, ((1, 1), (1, 1), (0, 0))))

def ssim_loss(mean_y, var_y, cov_xy, mean_x, var_x):
    top = (2.0 * mean_x * mean_y + ssim_one) * (2.0 * cov_xy + ssim_two)
    bottom = (mean_x * mean_x + mean_y * mean_y + ssim_one) * (var_x + var_y + ssim_two)
    return jnp.sum((1.0 - top / bottom) * 0.5)

def local_terms(xpad, ypad):
    mean_x = box_valid(xpad)
    mean_y = box_valid(ypad)
    var_x = box_valid(xpad * xpad) - mean_x * mean_x
    var_y = box_valid(ypad * ypad) - mean_y * mean_y
    cov_xy = box_valid(xpad * ypad) - mean_x * mean_y
    loss, pull = jax.vjp(lambda one, two, three: ssim_loss(one, two, three, mean_x, var_x), mean_y, var_y, cov_xy)
    grad_mean, grad_var, grad_cov = pull(jnp.ones_like(loss))
    first = grad_mean - 2.0 * grad_var * mean_y - grad_cov * mean_x
    return (first, grad_var, grad_cov)

def edge_weight(lower, upper):
    return jnp.exp(-lax.optimization_barrier(jnp.mean(jnp.abs(upper - lower), axis=-1)))

def charbonnier(weight, delta):
    return weight * delta / jnp.sqrt(delta * delta + charb_sq)

def reference(feat1, feat2):
    count = H * W
    queries = feat1.reshape(count, C)
    keys = feat2.reshape(count, C)
    where_at = jnp.arange(count, dtype=jnp.int32)
    coord_y = ((where_at // W).astype(jnp.float32) + 0.5) * (2.0 / H) - 1.0
    coord_x = ((where_at % W).astype(jnp.float32) + 0.5) * (2.0 / W) - 1.0
    scale = 1.0 / math.sqrt(C)
    block = math.gcd(count, 2048)

    def match(query_block):
        score = jnp.dot(query_block, keys.T, preferred_element_type=jnp.float32) * scale
        top = lax.optimization_barrier(jnp.max(score, axis=1, keepdims=True))
        expo = jnp.exp(score - top)
        total = lax.optimization_barrier(jnp.sum(expo, axis=1))
        mixed = jnp.dot(expo.astype(jnp.bfloat16), keys, preferred_element_type=jnp.float32) / total[:, None]
        along_y = lax.optimization_barrier(jnp.sum(expo * coord_y[None, :], axis=1)) / total
        along_x = lax.optimization_barrier(jnp.sum(expo * coord_x[None, :], axis=1)) / total
        return (mixed, along_y, along_x)
    mixed, along_y, along_x = lax.map(match, queries.reshape(count // block, block, C))
    warped = mixed.reshape(H, W, C).astype(jnp.bfloat16)
    flow = jnp.stack([along_y.reshape(count) - coord_y, along_x.reshape(count) - coord_x]).reshape(2, H, W)
    xval = feat1.astype(jnp.float32)
    yval = warped.astype(jnp.float32)
    pad_x = jnp.pad(xval, ((1, 1), (1, 1), (0, 0)))
    pad_y = jnp.pad(yval, ((1, 1), (1, 1), (0, 0)))
    first, grad_var, grad_cov = local_terms(pad_x, pad_y)
    grad_warped = box_zero(first) + 2.0 * yval * box_zero(grad_var) + xval * box_zero(grad_cov)
    weight_y = edge_weight(xval[:-1], xval[1:])
    delta_y = flow[:, 1:, :] - flow[:, :-1, :]
    push_y = charbonnier(weight_y[None], delta_y)
    weight_x = edge_weight(xval[:, :-1], xval[:, 1:])
    delta_x = flow[:, :, 1:] - flow[:, :, :-1]
    push_x = charbonnier(weight_x[None], delta_x)
    grad_flow = jnp.pad(push_y, ((0, 0), (1, 0), (0, 0))) - jnp.pad(push_y, ((0, 0), (0, 1), (0, 0)))
    grad_flow = grad_flow + jnp.pad(push_x, ((0, 0), (0, 0), (1, 0))) - jnp.pad(push_x, ((0, 0), (0, 0), (0, 1)))
    return (flow, grad_flow, grad_warped)
```

```python
import functools
import math

import jax
import jax.numpy as jnp
from jax import lax
from jax.experimental import pallas as pl
from jax.experimental.pallas import tpu as pltpu
from jax.sharding import PartitionSpec as P

ssim_one = 0.01
ssim_two = 0.03
charb_sq = 0.0001
SIDE = 8
MESH = pl.DeviceIdType.MESH


def gather_attend(
    nblk, ncol, f1, f2, x_out, y_out, c_out,
    keys, top_h, bot_h, left_h, right_h, xext, peak, acc, acc_c,
    recv, send_z, send_x, send_y, send_c, halo_send, halo_recv,
):
    rows, cols, width = f1.shape
    half_rows = rows // 2
    nz = nblk // 4
    i = lax.axis_index("blk")
    y = lax.axis_index("col")
    c = lax.rem(i, 2)
    x = lax.rem(i // 2, 2)
    z = i // 4

    def blk_of(zz, xx, cc):
        return (zz * 2 + xx) * 2 + cc

    def zmod(k):
        return lax.rem(z + k, nz)

    def ymod(k):
        return lax.rem(y + k, ncol)

    other_x = (blk_of(z, 1 - x, c), y)
    sibling = (blk_of(z, x, 1 - c), y)
    up, down = lax.rem(i + nblk - 1, nblk), lax.rem(i + 1, nblk)
    west, east = ymod(ncol - 1), ymod(1)

    keys[y, i] = f2[...]

    around = [(up, y), (down, y), (i, west), (i, east), (up, west), (up, east), (down, west), (down, east)]
    peers = [(blk_of(zmod(k), x, c), y) for k in range(1, nz)]
    peers += [(i, ymod(k)) for k in range(1, ncol)]
    peers += [other_x, sibling] + around
    barrier = pltpu.get_barrier_semaphore()
    for peer in peers:
        pl.semaphore_signal(barrier, inc=1, device_id=peer, device_id_type=MESH)
    pl.semaphore_wait(barrier, len(peers))

    def copy(yy, b, half, dest, sem):
        part = keys.at[yy, b, pl.ds(half * half_rows, half_rows)]
        return pltpu.make_async_remote_copy(
            src_ref=part, dst_ref=part, send_sem=sem, recv_sem=recv.at[yy, b, half],
            device_id=dest, device_id_type=MESH,
        )

    def arrived(yy, b, half):
        copy(yy, b, half, sibling, send_c.at[yy, b // 2, half]).wait_recv()

    def z_copy(k, half):
        return copy(y, i, half, (blk_of(zmod(k), x, c), y), send_z.at[k - 1, half])

    def x_copy(yy, zz, half):
        return copy(yy, blk_of(zz, x, c), half, other_x, send_x.at[half, yy, zz])

    def y_copy(k, zz, xx, half):
        return copy(y, blk_of(zz, xx, c), half, (i, ymod(k)), send_y.at[half, k - 1, zz, xx])

    def c_copy(yy, zz, xx, half):
        return copy(yy, blk_of(zz, xx, c), half, sibling, send_c.at[yy, zz * 2 + xx, half])

    def y_range(fn):
        if ncol == 2:
            fn(1)
        else:
            lax.fori_loop(1, ncol, lambda k, u: (fn(k), u)[1], 0)

    def z_range(low, fn):
        lax.fori_loop(low, nz, lambda k, u: (fn(k), u)[1], 0)

    def start_column(zz):
        x_copy(y, zz, 0).start()
        y_range(lambda k: y_copy(k, zz, x, 1).start())
        x_copy(y, zz, 1).start()
        y_range(lambda k: y_copy(k, zz, x, 0).start())
        c_copy(y, zz, x, 0).start()
        c_copy(y, zz, x, 1).start()

    def halo(src, dst, dest, n):
        return pltpu.make_async_remote_copy(
            src_ref=src, dst_ref=dst, send_sem=halo_send.at[n], recv_sem=halo_recv.at[n],
            device_id=dest, device_id_type=MESH,
        )

    first, last = pl.ds(0, 2), pl.ds(rows - 2, 2)
    lead, tail = pl.ds(0, 16), pl.ds(cols - 16, 16)
    mid, end = pl.ds(2, rows), pl.ds(rows + 2, 2)
    halos = [
        halo(f1.at[last], top_h, (down, y), 0),
        halo(f1.at[first], bot_h, (up, y), 1),
        halo(f1.at[:, tail], left_h.at[mid], (i, east), 2),
        halo(f1.at[:, lead], right_h.at[mid], (i, west), 3),
        halo(f1.at[last, tail], left_h.at[first], (down, east), 4),
        halo(f1.at[last, lead], right_h.at[first], (down, west), 5),
        halo(f1.at[first, tail], left_h.at[end], (up, east), 6),
        halo(f1.at[first, lead], right_h.at[end], (up, west), 7),
    ]

    for k in range(1, nz):
        z_copy(k, 0).start()
        z_copy(k, 1).start()
    for item in halos:
        item.start()
    start_column(z)

    peak[...] = jnp.full_like(peak, -1e30)
    acc[...] = jnp.zeros_like(acc)
    acc_c[...] = jnp.zeros_like(acc_c)
    per = 2 * rows * cols
    where = lax.broadcasted_iota(jnp.int32, (2 * rows, cols, 128), 0)
    along = lax.broadcasted_iota(jnp.int32, (2 * rows, cols, 128), 1)
    lane = lax.broadcasted_iota(jnp.int32, (2 * rows, cols, 128), 2)
    pattern = jnp.where(lane == 0, 1, jnp.where(lane == 1, where, jnp.where(lane == 2, along, 0)))
    pattern = pattern.astype(jnp.float32).reshape(per, 128)
    lane_row = lax.broadcasted_iota(jnp.int32, (1, 128), 1)

    for item in halos:
        item.wait_recv()
    xext[0:2, 0:cols] = top_h[...].astype(jnp.float32)
    xext[2 : rows + 2, 0:cols] = f1[...].astype(jnp.float32)
    xext[rows + 2 : rows + 4, 0:cols] = bot_h[...].astype(jnp.float32)
    spot = lax.broadcasted_iota(jnp.int32, (rows + 4, SIDE, width), 1)
    xext[:, cols : cols + SIDE] = jnp.where(
        spot < SIDE // 2,
        right_h[...].astype(jnp.float32)[:, 0:SIDE],
        left_h[...].astype(jnp.float32)[:, 16 - SIDE : 16],
    )
    count = (rows + 4) * (cols + SIDE)
    x_out[...] = xext[...].reshape(count, width).astype(jnp.bfloat16)
    scale = 1.0 / math.sqrt(width)

    def absorb(yy, zz, xx):
        chip = zz * 2 + xx
        for half in range(2):
            arrived(yy, chip * 2 + 1 - c, half)
        block = keys[yy, pl.ds(chip * 2, 2)].reshape(per, width)
        base = jnp.where(lane_row == 1, chip * 2 * rows, jnp.where(lane_row == 3, yy, 0))
        coords = (pattern + base.astype(jnp.float32)).astype(jnp.bfloat16)
        score = lax.dot_general(
            x_out[...], block, (((1,), (1,)), ((), ())), preferred_element_type=jnp.float32
        ) * scale
        old = peak[...]
        new = jnp.maximum(old, jnp.max(score, axis=1, keepdims=True))
        peak[...] = new
        shrink = jnp.exp(old - new)
        full = jnp.exp(score - new[:, 0:1])
        expo = full.astype(jnp.bfloat16)
        rest = (full - expo.astype(jnp.float32)).astype(jnp.bfloat16)
        acc[...] = acc[...] * shrink[:, 0:1] + jnp.dot(expo, block, preferred_element_type=jnp.float32)
        acc_c[...] = (
            acc_c[...] * shrink
            + jnp.dot(expo, coords, preferred_element_type=jnp.float32)
            + jnp.dot(rest, coords, preferred_element_type=jnp.float32)
        )

    absorb(y, z, x)

    def wave_z(k):
        zz = zmod(k)
        arrived(y, blk_of(zz, x, c), 0)
        arrived(y, blk_of(zz, x, c), 1)
        start_column(zz)

    z_range(1, wave_z)

    def wave_one(k):
        zz = zmod(k)
        arrived(y, blk_of(zz, 1 - x, c), 0)
        y_range(lambda j: y_copy(j, zz, 1 - x, 0).start())
        c_copy(y, zz, 1 - x, 0).start()

        def take(j):
            yy = ymod(j)
            arrived(yy, blk_of(zz, x, c), 1)
            x_copy(yy, zz, 1).start()
            c_copy(yy, zz, x, 1).start()

        y_range(take)

        @pl.when(k > 0)
        def _():
            absorb(y, zz, x)

    z_range(0, wave_one)

    def wave_two(k):
        zz = zmod(k)
        arrived(y, blk_of(zz, 1 - x, c), 1)
        c_copy(y, zz, 1 - x, 1).start()

        def take(j):
            yy = ymod(j)
            arrived(yy, blk_of(zz, x, c), 0)
            c_copy(yy, zz, x, 0).start()

        y_range(take)

        @pl.when(k > 0)
        def _():
            absorb(y, zmod(k + nz - 1), 1 - x)
            y_range(lambda j: absorb(ymod(j), zmod(k + nz - 1), x))

    z_range(0, wave_two)

    def wave_three(k):
        zz = zmod(k)

        def take(j):
            yy = ymod(j)
            arrived(yy, blk_of(zz, 1 - x, c), 0)
            c_copy(yy, zz, 1 - x, 0).start()
            arrived(yy, blk_of(zz, 1 - x, c), 1)
            c_copy(yy, zz, 1 - x, 1).start()

        y_range(take)

        @pl.when(k == 0)
        def _():
            absorb(y, zmod(nz - 1), 1 - x)
            y_range(lambda j: absorb(ymod(j), zmod(nz - 1), x))

        @pl.when(k > 0)
        def _():
            y_range(lambda j: absorb(ymod(j), zmod(k + nz - 1), 1 - x))

    z_range(0, wave_three)
    y_range(lambda j: absorb(ymod(j), zmod(nz - 1), 1 - x))

    total = acc_c[:, 0:1]
    y_out[...] = (acc[...] / total).astype(jnp.bfloat16)
    c_out[...] = acc_c[...] / total

    for item in halos:
        item.wait_send()
    for k in range(1, nz):
        z_copy(k, 0).wait_send()
        z_copy(k, 1).wait_send()

    def drain(zz):
        x_copy(y, zz, 0).wait_send()
        x_copy(y, zz, 1).wait_send()
        for xx in range(2):
            c_copy(y, zz, xx, 0).wait_send()
            c_copy(y, zz, xx, 1).wait_send()

        def each(j):
            yy = ymod(j)
            x_copy(yy, zz, 1).wait_send()
            y_copy(j, zz, x, 1).wait_send()
            for xx in range(2):
                y_copy(j, zz, xx, 0).wait_send()
                c_copy(yy, zz, xx, 0).wait_send()
                c_copy(yy, zz, xx, 1).wait_send()

        y_range(each)

    z_range(0, drain)


def col_sum(v):
    size = v.shape[1]
    return v + pltpu.roll(v, 1, 1) + pltpu.roll(v, size - 1, 1)


def box(v):
    n = v.shape[0]
    return col_sum(v[0 : n - 2] + v[1 : n - 1] + v[2:n]) * (1.0 / 9.0)


def turn(v, step):
    if step == 1:
        return jnp.concatenate([v[:, -1:], v[:, :-1]], axis=1)
    return jnp.concatenate([v[:, 1:], v[:, :1]], axis=1)


def charbonnier(weight, delta):
    return weight * delta / jnp.sqrt(delta * delta + charb_sq)


def stencil(nblk, ncol, rows, cols, x_ref, y_ref, c_ref, flow_ref, gflow_ref, grad_ref):
    width = x_ref.shape[1]
    span = cols + SIDE
    i = lax.axis_index("blk")
    y = lax.axis_index("col")
    full_rows, full_cols = rows * nblk, cols * ncol

    def place(shape, row_axis, col_axis, first_row):
        r = lax.broadcasted_iota(jnp.int32, shape, row_axis) + (i * rows + first_row)
        w = lax.broadcasted_iota(jnp.int32, shape, col_axis)
        w = jnp.where(w >= cols + SIDE // 2, w - span, w) + y * cols
        return r, w

    def inside(shape, first_row):
        r, w = place(shape, 0, 1, first_row)
        return (r >= 0) & (r < full_rows) & (w >= 0) & (w < full_cols)

    xraw = x_ref[...].astype(jnp.float32).reshape(rows + 4, span, width)
    keep = inside(xraw.shape, -2)
    xv = jnp.where(keep, xraw, 0.0)
    yv = jnp.where(keep, y_ref[...].astype(jnp.float32).reshape(rows + 4, span, width), 0.0)
    mx, my = box(xv), box(yv)
    vx = box(xv * xv) - mx * mx
    vy = box(yv * yv) - my * my
    cv = box(xv * yv) - mx * my
    n1 = 2.0 * mx * my + ssim_one
    n2 = 2.0 * cv + ssim_two
    d1 = mx * mx + my * my + ssim_one
    d2 = vx + vy + ssim_two
    inv1 = 1.0 / d1
    inv2 = 1.0 / d2
    inv = inv1 * inv2
    ssim = n1 * n2 * inv
    a = ssim * my * inv1 - mx * n2 * inv
    b = 0.5 * ssim * inv2
    cc = -n1 * inv
    first = a - 2.0 * b * my - cc * mx
    ok = inside(mx.shape, -1)
    g1 = box(jnp.where(ok, first, 0.0))
    g2 = box(jnp.where(ok, b, 0.0))
    g3 = box(jnp.where(ok, cc, 0.0))
    yc = yv[2 : rows + 2]
    xc = xv[2 : rows + 2]
    grad_ref[...] = (g1 + 2.0 * yc * g2 + xc * g3)[:, 0:cols]

    sums = jnp.transpose(c_ref[...])

    def plane(n):
        line = sums[n : n + 1]
        return jnp.concatenate([line[:, r * span : (r + 1) * span] for r in range(rows + 4)], axis=0)

    rr, ww = place((rows + 4, span), 0, 1, -2)
    fy = (plane(1) + 0.5) * (2.0 / full_rows) - 1.0 - ((rr.astype(jnp.float32) + 0.5) * (2.0 / full_rows) - 1.0)
    px = plane(2) + plane(3) * float(cols)
    fx = (px + 0.5) * (2.0 / full_cols) - 1.0 - ((ww.astype(jnp.float32) + 0.5) * (2.0 / full_cols) - 1.0)
    flow_ref[0] = fy[2 : rows + 2, 0:cols]
    flow_ref[1] = fx[2 : rows + 2, 0:cols]

    w_y = jnp.exp(-jnp.mean(jnp.abs(xraw[2 : rows + 3] - xraw[1 : rows + 2]), axis=-1))
    mid = xraw[2 : rows + 2]
    w_x = jnp.exp(-jnp.mean(jnp.abs(mid - pltpu.roll(mid, 1, 1)), axis=-1))
    er, _ = place((rows + 1, span), 0, 1, -1)
    use_y = (er >= 0) & (er <= full_rows - 2)
    _, ew = place((rows, span), 0, 1, 0)
    use_x = (ew >= 1) & (ew <= full_cols - 1)
    for n, f in enumerate((fy, fx)):
        push_y = jnp.where(use_y, charbonnier(w_y, f[2 : rows + 3] - f[1 : rows + 2]), 0.0)
        fm = f[2 : rows + 2]
        push_x = jnp.where(use_x, charbonnier(w_x, fm - turn(fm, 1)), 0.0)
        out = push_y[0:rows] - push_y[1 : rows + 1] + push_x - turn(push_x, -1)
        gflow_ref[n] = out[:, 0:cols]


def body(nblk, ncol, feat1, feat2):
    rows, cols, width = feat1.shape
    nz = nblk // 4
    count = (rows + 4) * (cols + SIDE)
    vmem = pl.BlockSpec(memory_space=pltpu.VMEM)
    dma = pltpu.SemaphoreType.DMA
    bf = jnp.bfloat16
    xq, warped, sums = pl.pallas_call(
        functools.partial(gather_attend, nblk, ncol),
        out_shape=(
            jax.ShapeDtypeStruct((count, width), bf),
            jax.ShapeDtypeStruct((count, width), bf),
            jax.ShapeDtypeStruct((count, 128), jnp.float32),
        ),
        in_specs=[vmem] * 2,
        out_specs=(vmem, vmem, vmem),
        scratch_shapes=[
            pltpu.VMEM((ncol, nblk, rows, cols, width), bf),
            pltpu.VMEM((2, cols, width), bf),
            pltpu.VMEM((2, cols, width), bf),
            pltpu.VMEM((rows + 4, 16, width), bf),
            pltpu.VMEM((rows + 4, 16, width), bf),
            pltpu.VMEM((rows + 4, cols + SIDE, width), jnp.float32),
            pltpu.VMEM((count, 128), jnp.float32),
            pltpu.VMEM((count, width), jnp.float32),
            pltpu.VMEM((count, 128), jnp.float32),
            dma((ncol, nblk, 2)),
            dma((nz - 1, 2)),
            dma((2, ncol, nz)),
            dma((2, ncol - 1, nz, 2)),
            dma((ncol, nblk // 2, 2)),
            dma((8,)),
            dma((8,)),
        ],
        compiler_params=pltpu.CompilerParams(
            collective_id=0, has_side_effects=True, vmem_limit_bytes=48 * 1024 * 1024
        ),
    )(feat1, feat2)
    return pl.pallas_call(
        functools.partial(stencil, nblk, ncol, rows, cols),
        out_shape=(
            jax.ShapeDtypeStruct((2, rows, cols), jnp.float32),
            jax.ShapeDtypeStruct((2, rows, cols), jnp.float32),
            jax.ShapeDtypeStruct((rows, cols, width), jnp.float32),
        ),
        in_specs=[vmem] * 3,
        out_specs=(vmem, vmem, vmem),
        compiler_params=pltpu.CompilerParams(vmem_limit_bytes=40 * 1024 * 1024),
    )(xq, warped, sums)


def solution(mesh):
    placed = (P("blk", "col", None), P("blk", "col", None))
    return jax.shard_map(
        functools.partial(body, mesh.shape["blk"], mesh.shape["col"]),
        mesh=mesh,
        in_specs=placed,
        out_specs=(P(None, "blk", "col"), P(None, "blk", "col"), P("blk", "col", None)),
        check_vma=False,
    )
```

```python
import functools
import math

import jax
import jax.numpy as jnp
from jax import lax
from jax.experimental import pallas as pl
from jax.experimental.pallas import tpu as pltpu
from jax.sharding import PartitionSpec as P

ssim_one = 0.01
ssim_two = 0.03
charb_sq = 0.0001
SIDE = 8
MESH = pl.DeviceIdType.MESH


def gather_attend(
    nblk, ncol, f1, f2, x_out, y_out, c_out,
    keys, x_bufs, y_bufs, c_bufs, own_y, own_c, query, ext, ext_c, peak, acc, acc_c,
    recv, send_z, send_x, send_y, send_c, halo_send, halo_recv,
):
    rows, cols, width = f1.shape
    half_rows = rows // 2
    nz = nblk // 4
    i = lax.axis_index("blk")
    y = lax.axis_index("col")
    c = lax.rem(i, 2)
    x = lax.rem(i // 2, 2)
    z = i // 4

    def blk_of(zz, xx, cc):
        return (zz * 2 + xx) * 2 + cc

    def zmod(k):
        return lax.rem(z + k, nz)

    def ymod(k):
        return lax.rem(y + k, ncol)

    other_x = (blk_of(z, 1 - x, c), y)
    sibling = (blk_of(z, x, 1 - c), y)
    up, down = lax.rem(i + nblk - 1, nblk), lax.rem(i + 1, nblk)
    west, east = ymod(ncol - 1), ymod(1)

    keys[y, i] = f2[...]

    around = [(up, y), (down, y), (i, west), (i, east), (up, west), (up, east), (down, west), (down, east)]
    peers = [(blk_of(zmod(k), x, c), y) for k in range(1, nz)]
    peers += [(i, ymod(k)) for k in range(1, ncol)]
    peers += [other_x, sibling] + around
    barrier = pltpu.get_barrier_semaphore()
    for peer in peers:
        pl.semaphore_signal(barrier, inc=1, device_id=peer, device_id_type=MESH)
    pl.semaphore_wait(barrier, len(peers))

    def copy(yy, b, half, dest, sem):
        part = keys.at[yy, b, pl.ds(half * half_rows, half_rows)]
        return pltpu.make_async_remote_copy(
            src_ref=part, dst_ref=part, send_sem=sem, recv_sem=recv.at[yy, b, half],
            device_id=dest, device_id_type=MESH,
        )

    def arrived(yy, b, half):
        copy(yy, b, half, sibling, send_c.at[yy, b // 2, half]).wait_recv()

    def z_copy(k, half):
        return copy(y, i, half, (blk_of(zmod(k), x, c), y), send_z.at[k - 1, half])

    def x_copy(yy, zz, half):
        return copy(yy, blk_of(zz, x, c), half, other_x, send_x.at[half, yy, zz])

    def y_copy(k, zz, xx, half):
        return copy(y, blk_of(zz, xx, c), half, (i, ymod(k)), send_y.at[half, k - 1, zz, xx])

    def c_copy(yy, zz, xx, half):
        return copy(yy, blk_of(zz, xx, c), half, sibling, send_c.at[yy, zz * 2 + xx, half])

    def y_range(fn):
        if ncol == 2:
            fn(1)
        else:
            lax.fori_loop(1, ncol, lambda k, u: (fn(k), u)[1], 0)

    def z_range(low, fn):
        lax.fori_loop(low, nz, lambda k, u: (fn(k), u)[1], 0)

    def start_column(zz):
        x_copy(y, zz, 0).start()
        y_range(lambda k: y_copy(k, zz, x, 1).start())
        x_copy(y, zz, 1).start()
        y_range(lambda k: y_copy(k, zz, x, 0).start())
        c_copy(y, zz, x, 0).start()
        c_copy(y, zz, x, 1).start()

    def halo(src, dst, dest, n):
        return pltpu.make_async_remote_copy(
            src_ref=src, dst_ref=dst, send_sem=halo_send.at[n], recv_sem=halo_recv.at[n],
            device_id=dest, device_id_type=MESH,
        )

    first, last = pl.ds(0, 2), pl.ds(rows - 2, 2)
    lead, tail = pl.ds(0, 16), pl.ds(cols - 16, 16)
    mid, end = pl.ds(2, rows), pl.ds(rows + 2, 2)
    def eight(src, bufs, at):
        top_h, bot_h, left_h, right_h = bufs
        return [
            halo(src.at[last], top_h, (down, y), at),
            halo(src.at[first], bot_h, (up, y), at + 1),
            halo(src.at[:, tail], left_h.at[mid], (i, east), at + 2),
            halo(src.at[:, lead], right_h.at[mid], (i, west), at + 3),
            halo(src.at[last, tail], left_h.at[first], (down, east), at + 4),
            halo(src.at[last, lead], right_h.at[first], (down, west), at + 5),
            halo(src.at[first, tail], left_h.at[end], (up, east), at + 6),
            halo(src.at[first, lead], right_h.at[end], (up, west), at + 7),
        ]

    halos = eight(f1, x_bufs, 0)
    late = [
        halo(own_c.at[pl.ds(rows - 1, 1)], c_bufs[0], (down, y), 16),
        halo(own_c.at[pl.ds(0, 1)], c_bufs[1], (up, y), 17),
        halo(own_c.at[:, pl.ds(cols - SIDE, SIDE)], c_bufs[2], (i, east), 18),
        halo(own_c.at[:, pl.ds(0, SIDE)], c_bufs[3], (i, west), 19),
    ] + eight(own_y, y_bufs, 8)

    for k in range(1, nz):
        z_copy(k, 0).start()
        z_copy(k, 1).start()
    for item in halos:
        item.start()
    start_column(z)

    peak[...] = jnp.full_like(peak, -1e30)
    acc[...] = jnp.zeros_like(acc)
    acc_c[...] = jnp.zeros_like(acc_c)
    per = 2 * rows * cols
    where = lax.broadcasted_iota(jnp.int32, (2 * rows, cols, 128), 0)
    along = lax.broadcasted_iota(jnp.int32, (2 * rows, cols, 128), 1)
    lane = lax.broadcasted_iota(jnp.int32, (2 * rows, cols, 128), 2)
    pattern = jnp.where(lane == 0, 1, jnp.where(lane == 1, where, jnp.where(lane == 2, along, 0)))
    pattern = pattern.astype(jnp.float32).reshape(per, 128)
    lane_row = lax.broadcasted_iota(jnp.int32, (1, 128), 1)

    count = (rows + 4) * (cols + SIDE)
    scale = 1.0 / math.sqrt(width)
    query[...] = (f1[...].astype(jnp.float32) * scale).reshape(rows * cols, width).astype(jnp.bfloat16)

    def widen(own, bufs):
        top_h, bot_h, left_h, right_h = bufs
        ext[0:2, 0:cols] = top_h[...].astype(jnp.float32)
        ext[2 : rows + 2, 0:cols] = own[...].astype(jnp.float32)
        ext[rows + 2 : rows + 4, 0:cols] = bot_h[...].astype(jnp.float32)
        spot = lax.broadcasted_iota(jnp.int32, (rows + 4, SIDE, width), 1)
        ext[:, cols : cols + SIDE] = jnp.where(
            spot < SIDE // 2,
            right_h[...].astype(jnp.float32)[:, 0:SIDE],
            left_h[...].astype(jnp.float32)[:, 16 - SIDE : 16],
        )
        return ext[...].reshape(count, width).astype(jnp.bfloat16)

    def absorb(*chips):
        blocks, coords, scores = [], [], []
        for yy, zz, xx in chips:
            chip = zz * 2 + xx
            for half in range(2):
                arrived(yy, chip * 2 + 1 - c, half)
            block = keys[yy, pl.ds(chip * 2, 2)].reshape(per, width)
            base = jnp.where(lane_row == 1, chip * 2 * rows, jnp.where(lane_row == 3, yy, 0))
            blocks.append(block)
            coords.append((pattern + base.astype(jnp.float32)).astype(jnp.bfloat16))
            scores.append(
                lax.dot_general(
                    query[...], block, (((1,), (1,)), ((), ())), preferred_element_type=jnp.float32
                )
            )
        old = peak[...]
        new = old
        for score in scores:
            new = jnp.maximum(new, jnp.max(score, axis=1, keepdims=True))
        peak[...] = new
        shrink = jnp.exp(old - new)
        mixed = acc[...] * shrink[:, 0:1]
        placed = acc_c[...] * shrink
        for block, coord, score in zip(blocks, coords, scores):
            full = jnp.exp(score - new[:, 0:1])
            expo = full.astype(jnp.bfloat16)
            rest = (full - expo.astype(jnp.float32)).astype(jnp.bfloat16)
            mixed = mixed + jnp.dot(expo, block, preferred_element_type=jnp.float32)
            placed = placed + jnp.dot(expo, coord, preferred_element_type=jnp.float32)
            placed = placed + jnp.dot(rest, coord, preferred_element_type=jnp.float32)
        acc[...] = mixed
        acc_c[...] = placed

    def absorb_two(zz):
        if ncol == 2:
            absorb((y, zz, 1 - x), (1 - y, zz, x))
        else:
            absorb((y, zz, 1 - x))
            y_range(lambda j: absorb((ymod(j), zz, x)))

    absorb((y, z, x))

    def wave_z(k):
        zz = zmod(k)
        arrived(y, blk_of(zz, x, c), 0)
        arrived(y, blk_of(zz, x, c), 1)
        start_column(zz)

    z_range(1, wave_z)

    def wave_one(k):
        zz = zmod(k)
        arrived(y, blk_of(zz, 1 - x, c), 0)
        y_range(lambda j: y_copy(j, zz, 1 - x, 0).start())
        c_copy(y, zz, 1 - x, 0).start()

        def take(j):
            yy = ymod(j)
            arrived(yy, blk_of(zz, x, c), 1)
            x_copy(yy, zz, 1).start()
            c_copy(yy, zz, x, 1).start()

        y_range(take)

        @pl.when(k > 0)
        def _():
            absorb((y, zz, x))

    z_range(0, wave_one)

    def wave_two(k):
        zz = zmod(k)
        arrived(y, blk_of(zz, 1 - x, c), 1)
        c_copy(y, zz, 1 - x, 1).start()

        def take(j):
            yy = ymod(j)
            arrived(yy, blk_of(zz, x, c), 0)
            c_copy(yy, zz, x, 0).start()

        y_range(take)

        @pl.when(k > 0)
        def _():
            absorb_two(zmod(k + nz - 1))

    z_range(0, wave_two)

    def wave_three(k):
        zz = zmod(k)

        def take(j):
            yy = ymod(j)
            arrived(yy, blk_of(zz, 1 - x, c), 0)
            c_copy(yy, zz, 1 - x, 0).start()
            arrived(yy, blk_of(zz, 1 - x, c), 1)
            c_copy(yy, zz, 1 - x, 1).start()

        y_range(take)

        @pl.when(k == 0)
        def _():
            absorb_two(zmod(nz - 1))

        @pl.when(k > 0)
        def _():
            y_range(lambda j: absorb((ymod(j), zmod(k + nz - 1), 1 - x)))

    z_range(0, wave_three)
    y_range(lambda j: absorb((ymod(j), zmod(nz - 1), 1 - x)))

    total = acc_c[:, 0:1]
    own_c[...] = (acc_c[...] / total).reshape(rows, cols, 128)
    own_y[...] = (acc[...] / total).reshape(rows, cols, width).astype(jnp.bfloat16)
    for item in late:
        item.start()
    for item in halos:
        item.wait_recv()
    x_out[...] = widen(f1, x_bufs)
    ext_c[...] = jnp.zeros_like(ext_c)
    ext_c[2 : rows + 2, 0:cols] = own_c[...]
    for item in late:
        item.wait_recv()
    ext_c[1:2, 0:cols] = c_bufs[0][...]
    ext_c[rows + 2 : rows + 3, 0:cols] = c_bufs[1][...]
    spot_c = lax.broadcasted_iota(jnp.int32, (rows, SIDE, 128), 1)
    ext_c[2 : rows + 2, cols : cols + SIDE] = jnp.where(
        spot_c < SIDE // 2, c_bufs[3][...], c_bufs[2][...]
    )
    c_out[...] = ext_c[...].reshape(count, 128)
    y_out[...] = widen(own_y, y_bufs)

    for item in late:
        item.wait_send()
    for item in halos:
        item.wait_send()
    for k in range(1, nz):
        z_copy(k, 0).wait_send()
        z_copy(k, 1).wait_send()

    def drain(zz):
        x_copy(y, zz, 0).wait_send()
        x_copy(y, zz, 1).wait_send()
        for xx in range(2):
            c_copy(y, zz, xx, 0).wait_send()
            c_copy(y, zz, xx, 1).wait_send()

        def each(j):
            yy = ymod(j)
            x_copy(yy, zz, 1).wait_send()
            y_copy(j, zz, x, 1).wait_send()
            for xx in range(2):
                y_copy(j, zz, xx, 0).wait_send()
                c_copy(yy, zz, xx, 0).wait_send()
                c_copy(yy, zz, xx, 1).wait_send()

        y_range(each)

    z_range(0, drain)


def col_sum(v):
    size = v.shape[1]
    return v + pltpu.roll(v, 1, 1) + pltpu.roll(v, size - 1, 1)


def box(v):
    n = v.shape[0]
    return col_sum(v[0 : n - 2] + v[1 : n - 1] + v[2:n]) * (1.0 / 9.0)


def turn(v, step):
    if step == 1:
        return jnp.concatenate([v[:, -1:], v[:, :-1]], axis=1)
    return jnp.concatenate([v[:, 1:], v[:, :1]], axis=1)


def charbonnier(weight, delta):
    return weight * delta / jnp.sqrt(delta * delta + charb_sq)


def stencil(nblk, ncol, rows, cols, x_ref, y_ref, c_ref, flow_ref, gflow_ref, grad_ref):
    width = x_ref.shape[1]
    span = cols + SIDE
    i = lax.axis_index("blk")
    y = lax.axis_index("col")
    full_rows, full_cols = rows * nblk, cols * ncol

    def place(shape, row_axis, col_axis, first_row):
        r = lax.broadcasted_iota(jnp.int32, shape, row_axis) + (i * rows + first_row)
        w = lax.broadcasted_iota(jnp.int32, shape, col_axis)
        w = jnp.where(w >= cols + SIDE // 2, w - span, w) + y * cols
        return r, w

    def inside(shape, first_row):
        r, w = place(shape, 0, 1, first_row)
        return (r >= 0) & (r < full_rows) & (w >= 0) & (w < full_cols)

    xraw = x_ref[...].astype(jnp.float32).reshape(rows + 4, span, width)
    keep = inside(xraw.shape, -2)
    xv = jnp.where(keep, xraw, 0.0)
    yv = jnp.where(keep, y_ref[...].astype(jnp.float32).reshape(rows + 4, span, width), 0.0)
    mx, my = box(xv), box(yv)
    vx = box(xv * xv) - mx * mx
    vy = box(yv * yv) - my * my
    cv = box(xv * yv) - mx * my
    n1 = 2.0 * mx * my + ssim_one
    n2 = 2.0 * cv + ssim_two
    d1 = mx * mx + my * my + ssim_one
    d2 = vx + vy + ssim_two
    inv1 = 1.0 / d1
    inv2 = 1.0 / d2
    inv = inv1 * inv2
    ssim = n1 * n2 * inv
    a = ssim * my * inv1 - mx * n2 * inv
    b = 0.5 * ssim * inv2
    cc = -n1 * inv
    first = a - 2.0 * b * my - cc * mx
    ok = inside(mx.shape, -1)
    g1 = box(jnp.where(ok, first, 0.0))
    g2 = box(jnp.where(ok, b, 0.0))
    g3 = box(jnp.where(ok, cc, 0.0))
    yc = yv[2 : rows + 2]
    xc = xv[2 : rows + 2]
    grad_ref[...] = (g1 + 2.0 * yc * g2 + xc * g3)[:, 0:cols]

    sums = jnp.transpose(c_ref[...])

    def plane(n):
        line = sums[n : n + 1]
        return jnp.concatenate([line[:, r * span : (r + 1) * span] for r in range(rows + 4)], axis=0)

    rr, ww = place((rows + 4, span), 0, 1, -2)
    fy = (plane(1) + 0.5) * (2.0 / full_rows) - 1.0 - ((rr.astype(jnp.float32) + 0.5) * (2.0 / full_rows) - 1.0)
    px = plane(2) + plane(3) * float(cols)
    fx = (px + 0.5) * (2.0 / full_cols) - 1.0 - ((ww.astype(jnp.float32) + 0.5) * (2.0 / full_cols) - 1.0)
    flow_ref[0] = fy[2 : rows + 2, 0:cols]
    flow_ref[1] = fx[2 : rows + 2, 0:cols]

    w_y = jnp.exp(-jnp.mean(jnp.abs(xraw[2 : rows + 3] - xraw[1 : rows + 2]), axis=-1))
    mid = xraw[2 : rows + 2]
    w_x = jnp.exp(-jnp.mean(jnp.abs(mid - pltpu.roll(mid, 1, 1)), axis=-1))
    er, _ = place((rows + 1, span), 0, 1, -1)
    use_y = (er >= 0) & (er <= full_rows - 2)
    _, ew = place((rows, span), 0, 1, 0)
    use_x = (ew >= 1) & (ew <= full_cols - 1)
    for n, f in enumerate((fy, fx)):
        push_y = jnp.where(use_y, charbonnier(w_y, f[2 : rows + 3] - f[1 : rows + 2]), 0.0)
        fm = f[2 : rows + 2]
        push_x = jnp.where(use_x, charbonnier(w_x, fm - turn(fm, 1)), 0.0)
        out = push_y[0:rows] - push_y[1 : rows + 1] + push_x - turn(push_x, -1)
        gflow_ref[n] = out[:, 0:cols]


def body(nblk, ncol, feat1, feat2):
    rows, cols, width = feat1.shape
    nz = nblk // 4
    count = (rows + 4) * (cols + SIDE)
    vmem = pl.BlockSpec(memory_space=pltpu.VMEM)
    dma = pltpu.SemaphoreType.DMA
    bf = jnp.bfloat16
    edges = (
        pltpu.VMEM((2, cols, width), bf),
        pltpu.VMEM((2, cols, width), bf),
        pltpu.VMEM((rows + 4, 16, width), bf),
        pltpu.VMEM((rows + 4, 16, width), bf),
    )
    xq, warped, sums = pl.pallas_call(
        functools.partial(gather_attend, nblk, ncol),
        out_shape=(
            jax.ShapeDtypeStruct((count, width), bf),
            jax.ShapeDtypeStruct((count, width), bf),
            jax.ShapeDtypeStruct((count, 128), jnp.float32),
        ),
        in_specs=[vmem] * 2,
        out_specs=(vmem, vmem, vmem),
        scratch_shapes=[
            pltpu.VMEM((ncol, nblk, rows, cols, width), bf),
            edges,
            edges,
            (
                pltpu.VMEM((1, cols, 128), jnp.float32),
                pltpu.VMEM((1, cols, 128), jnp.float32),
                pltpu.VMEM((rows, SIDE, 128), jnp.float32),
                pltpu.VMEM((rows, SIDE, 128), jnp.float32),
            ),
            pltpu.VMEM((rows, cols, width), bf),
            pltpu.VMEM((rows, cols, 128), jnp.float32),
            pltpu.VMEM((rows * cols, width), bf),
            pltpu.VMEM((rows + 4, cols + SIDE, width), jnp.float32),
            pltpu.VMEM((rows + 4, cols + SIDE, 128), jnp.float32),
            pltpu.VMEM((rows * cols, 128), jnp.float32),
            pltpu.VMEM((rows * cols, width), jnp.float32),
            pltpu.VMEM((rows * cols, 128), jnp.float32),
            dma((ncol, nblk, 2)),
            dma((nz - 1, 2)),
            dma((2, ncol, nz)),
            dma((2, ncol - 1, nz, 2)),
            dma((ncol, nblk // 2, 2)),
            dma((20,)),
            dma((20,)),
        ],
        compiler_params=pltpu.CompilerParams(
            collective_id=0, has_side_effects=True, vmem_limit_bytes=48 * 1024 * 1024
        ),
    )(feat1, feat2)
    return pl.pallas_call(
        functools.partial(stencil, nblk, ncol, rows, cols),
        out_shape=(
            jax.ShapeDtypeStruct((2, rows, cols), jnp.float32),
            jax.ShapeDtypeStruct((2, rows, cols), jnp.float32),
            jax.ShapeDtypeStruct((rows, cols, width), jnp.float32),
        ),
        in_specs=[vmem] * 3,
        out_specs=(vmem, vmem, vmem),
        compiler_params=pltpu.CompilerParams(vmem_limit_bytes=40 * 1024 * 1024),
    )(xq, warped, sums)


def solution(mesh):
    placed = (P("blk", "col", None), P("blk", "col", None))
    return jax.shard_map(
        functools.partial(body, mesh.shape["blk"], mesh.shape["col"]),
        mesh=mesh,
        in_specs=placed,
        out_specs=(P(None, "blk", "col"), P(None, "blk", "col"), P("blk", "col", None)),
        check_vma=False,
    )
```

```python
import functools
import math

import jax
import jax.numpy as jnp
from jax import lax
from jax.experimental import pallas as pl
from jax.experimental.pallas import tpu as pltpu
from jax.sharding import PartitionSpec as P

ssim_one = 0.01
ssim_two = 0.03
charb_sq = 0.0001
SIDE = 8
MESH = pl.DeviceIdType.MESH


def gather_attend(
    nblk, ncol, f1, f2, x_out, y_out, c_out,
    keys, x_bufs, y_bufs, c_bufs, own_y, own_c, query, ext, ext_c, peak, acc, acc_c,
    recv, send_z, send_x, send_y, send_c, halo_send, halo_recv,
):
    rows, cols, width = f1.shape
    half_rows = rows // 2
    nz = nblk // 4
    i = lax.axis_index("blk")
    y = lax.axis_index("col")
    c = lax.rem(i, 2)
    x = lax.rem(i // 2, 2)
    z = i // 4

    def blk_of(zz, xx, cc):
        return (zz * 2 + xx) * 2 + cc

    def zmod(k):
        if nz & (nz - 1):
            return lax.rem(z + k, nz)
        found = 0
        for bit in range(nz.bit_length() - 1):
            step = 2**bit
            found = found + lax.rem(z // step + k // step, 2) * step
        return found

    def ymod(k):
        return lax.rem(y + k, ncol)

    other_x = (blk_of(z, 1 - x, c), y)
    sibling = (blk_of(z, x, 1 - c), y)
    up, down = lax.rem(i + nblk - 1, nblk), lax.rem(i + 1, nblk)
    west, east = ymod(ncol - 1), ymod(1)

    keys[y, i] = f2[...]

    around = [(up, y), (down, y), (i, west), (i, east), (up, west), (up, east), (down, west), (down, east)]
    peers = [(blk_of(zmod(k), x, c), y) for k in range(1, nz)]
    peers += [(i, ymod(k)) for k in range(1, ncol)]
    peers += [other_x, sibling] + around
    barrier = pltpu.get_barrier_semaphore()
    for peer in peers:
        pl.semaphore_signal(barrier, inc=1, device_id=peer, device_id_type=MESH)
    pl.semaphore_wait(barrier, len(peers))

    def copy(yy, b, half, dest, sem):
        part = keys.at[yy, b, pl.ds(half * half_rows, half_rows)]
        return pltpu.make_async_remote_copy(
            src_ref=part, dst_ref=part, send_sem=sem, recv_sem=recv.at[yy, b, half],
            device_id=dest, device_id_type=MESH,
        )

    def arrived(yy, b, half):
        copy(yy, b, half, sibling, send_c.at[yy, b // 2, half]).wait_recv()

    def z_copy(k, half):
        return copy(y, i, half, (blk_of(zmod(k), x, c), y), send_z.at[k - 1, half])

    def x_copy(yy, zz, half):
        return copy(yy, blk_of(zz, x, c), half, other_x, send_x.at[half, yy, zz])

    def y_copy(k, zz, xx, half):
        return copy(y, blk_of(zz, xx, c), half, (i, ymod(k)), send_y.at[half, k - 1, zz, xx])

    def c_copy(yy, zz, xx, half):
        return copy(yy, blk_of(zz, xx, c), half, sibling, send_c.at[yy, zz * 2 + xx, half])

    def y_range(fn):
        if ncol == 2:
            fn(1)
        else:
            lax.fori_loop(1, ncol, lambda k, u: (fn(k), u)[1], 0)

    def z_range(low, fn):
        lax.fori_loop(low, nz, lambda k, u: (fn(k), u)[1], 0)

    def start_column(zz):
        x_copy(y, zz, 0).start()
        y_range(lambda k: y_copy(k, zz, x, 1).start())
        x_copy(y, zz, 1).start()
        y_range(lambda k: y_copy(k, zz, x, 0).start())
        c_copy(y, zz, x, 0).start()
        c_copy(y, zz, x, 1).start()

    def halo(src, dst, dest, n):
        return pltpu.make_async_remote_copy(
            src_ref=src, dst_ref=dst, send_sem=halo_send.at[n], recv_sem=halo_recv.at[n],
            device_id=dest, device_id_type=MESH,
        )

    first, last = pl.ds(0, 2), pl.ds(rows - 2, 2)
    lead, tail = pl.ds(0, 16), pl.ds(cols - 16, 16)
    mid, end = pl.ds(2, rows), pl.ds(rows + 2, 2)
    def eight(src, bufs, at):
        top_h, bot_h, left_h, right_h = bufs
        return [
            halo(src.at[last], top_h, (down, y), at),
            halo(src.at[first], bot_h, (up, y), at + 1),
            halo(src.at[:, tail], left_h.at[mid], (i, east), at + 2),
            halo(src.at[:, lead], right_h.at[mid], (i, west), at + 3),
            halo(src.at[last, tail], left_h.at[first], (down, east), at + 4),
            halo(src.at[last, lead], right_h.at[first], (down, west), at + 5),
            halo(src.at[first, tail], left_h.at[end], (up, east), at + 6),
            halo(src.at[first, lead], right_h.at[end], (up, west), at + 7),
        ]

    halos = eight(f1, x_bufs, 0)
    late = [
        halo(own_c.at[pl.ds(rows - 1, 1)], c_bufs[0], (down, y), 16),
        halo(own_c.at[pl.ds(0, 1)], c_bufs[1], (up, y), 17),
        halo(own_c.at[:, pl.ds(cols - SIDE, SIDE)], c_bufs[2], (i, east), 18),
        halo(own_c.at[:, pl.ds(0, SIDE)], c_bufs[3], (i, west), 19),
    ] + eight(own_y, y_bufs, 8)

    for k in range(1, nz):
        z_copy(k, 0).start()
        z_copy(k, 1).start()
    for item in halos:
        item.start()
    start_column(z)

    peak[...] = jnp.full_like(peak, -1e30)
    acc[...] = jnp.zeros_like(acc)
    acc_c[...] = jnp.zeros_like(acc_c)
    per = 2 * rows * cols
    where = lax.broadcasted_iota(jnp.int32, (2 * rows, cols, 128), 0)
    along = lax.broadcasted_iota(jnp.int32, (2 * rows, cols, 128), 1)
    lane = lax.broadcasted_iota(jnp.int32, (2 * rows, cols, 128), 2)
    pattern = jnp.where(lane == 0, 1, jnp.where(lane == 1, where, jnp.where(lane == 2, along, 0)))
    pattern = pattern.astype(jnp.float32).reshape(per, 128)
    lane_row = lax.broadcasted_iota(jnp.int32, (1, 128), 1)

    count = (rows + 4) * (cols + SIDE)
    scale = 1.0 / math.sqrt(width)
    query[...] = (f1[...].astype(jnp.float32) * scale).reshape(rows * cols, width).astype(jnp.bfloat16)

    def widen(own, bufs):
        top_h, bot_h, left_h, right_h = bufs
        ext[0:2, 0:cols] = top_h[...].astype(jnp.float32)
        ext[2 : rows + 2, 0:cols] = own[...].astype(jnp.float32)
        ext[rows + 2 : rows + 4, 0:cols] = bot_h[...].astype(jnp.float32)
        spot = lax.broadcasted_iota(jnp.int32, (rows + 4, SIDE, width), 1)
        ext[:, cols : cols + SIDE] = jnp.where(
            spot < SIDE // 2,
            right_h[...].astype(jnp.float32)[:, 0:SIDE],
            left_h[...].astype(jnp.float32)[:, 16 - SIDE : 16],
        )
        return ext[...].reshape(count, width).astype(jnp.bfloat16)

    def absorb(*chips):
        blocks, coords, scores = [], [], []
        for yy, zz, xx in chips:
            chip = zz * 2 + xx
            for half in range(2):
                arrived(yy, chip * 2 + 1 - c, half)
            block = keys[yy, pl.ds(chip * 2, 2)].reshape(per, width)
            base = jnp.where(lane_row == 1, chip * 2 * rows, jnp.where(lane_row == 3, yy, 0))
            blocks.append(block)
            coords.append((pattern + base.astype(jnp.float32)).astype(jnp.bfloat16))
            scores.append(
                lax.dot_general(
                    query[...], block, (((1,), (1,)), ((), ())), preferred_element_type=jnp.float32
                )
            )
        old = peak[...]
        new = old
        for score in scores:
            new = jnp.maximum(new, jnp.max(score, axis=1, keepdims=True))
        peak[...] = new
        shrink = jnp.exp(old - new)
        mixed = acc[...] * shrink[:, 0:1]
        placed = acc_c[...] * shrink
        for block, coord, score in zip(blocks, coords, scores):
            full = jnp.exp(score - new[:, 0:1])
            expo = full.astype(jnp.bfloat16)
            rest = (full - expo.astype(jnp.float32)).astype(jnp.bfloat16)
            mixed = mixed + jnp.dot(expo, block, preferred_element_type=jnp.float32)
            placed = placed + jnp.dot(expo, coord, preferred_element_type=jnp.float32)
            placed = placed + jnp.dot(rest, coord, preferred_element_type=jnp.float32)
        acc[...] = mixed
        acc_c[...] = placed

    def absorb_two(zz):
        if ncol == 2:
            absorb((y, zz, 1 - x), (1 - y, zz, x))
        else:
            absorb((y, zz, 1 - x))
            y_range(lambda j: absorb((ymod(j), zz, x)))

    absorb((y, z, x))

    def wave_z(k):
        zz = zmod(k)
        arrived(y, blk_of(zz, x, c), 0)
        arrived(y, blk_of(zz, x, c), 1)
        start_column(zz)

    z_range(1, wave_z)

    def wave_one(k):
        zz = zmod(k)
        arrived(y, blk_of(zz, 1 - x, c), 0)
        y_range(lambda j: y_copy(j, zz, 1 - x, 0).start())
        c_copy(y, zz, 1 - x, 0).start()

        def take(j):
            yy = ymod(j)
            arrived(yy, blk_of(zz, x, c), 1)
            x_copy(yy, zz, 1).start()
            c_copy(yy, zz, x, 1).start()

        y_range(take)

        @pl.when(k > 0)
        def _():
            absorb((y, zz, x))

    z_range(0, wave_one)

    def wave_two(k):
        zz = zmod(k)
        arrived(y, blk_of(zz, 1 - x, c), 1)
        c_copy(y, zz, 1 - x, 1).start()

        def take(j):
            yy = ymod(j)
            arrived(yy, blk_of(zz, x, c), 0)
            c_copy(yy, zz, x, 0).start()

        y_range(take)

        @pl.when(k > 0)
        def _():
            absorb_two(zmod(k - 1))

    z_range(0, wave_two)

    def wave_three(k):
        zz = zmod(k)

        def take(j):
            yy = ymod(j)
            arrived(yy, blk_of(zz, 1 - x, c), 0)
            c_copy(yy, zz, 1 - x, 0).start()
            arrived(yy, blk_of(zz, 1 - x, c), 1)
            c_copy(yy, zz, 1 - x, 1).start()

        y_range(take)

        @pl.when(k == 0)
        def _():
            absorb_two(zmod(nz - 1))

        @pl.when(k > 0)
        def _():
            y_range(lambda j: absorb((ymod(j), zmod(k - 1), 1 - x)))

    z_range(0, wave_three)
    y_range(lambda j: absorb((ymod(j), zmod(nz - 1), 1 - x)))

    total = acc_c[:, 0:1]
    own_c[...] = (acc_c[...] / total).reshape(rows, cols, 128)
    own_y[...] = (acc[...] / total).reshape(rows, cols, width).astype(jnp.bfloat16)
    for item in late:
        item.start()
    for item in halos:
        item.wait_recv()
    x_out[...] = widen(f1, x_bufs)
    ext_c[...] = jnp.zeros_like(ext_c)
    ext_c[2 : rows + 2, 0:cols] = own_c[...]
    for item in late:
        item.wait_recv()
    ext_c[1:2, 0:cols] = c_bufs[0][...]
    ext_c[rows + 2 : rows + 3, 0:cols] = c_bufs[1][...]
    spot_c = lax.broadcasted_iota(jnp.int32, (rows, SIDE, 128), 1)
    ext_c[2 : rows + 2, cols : cols + SIDE] = jnp.where(
        spot_c < SIDE // 2, c_bufs[3][...], c_bufs[2][...]
    )
    c_out[...] = ext_c[...].reshape(count, 128)
    y_out[...] = widen(own_y, y_bufs)

    for item in late:
        item.wait_send()
    for item in halos:
        item.wait_send()
    for k in range(1, nz):
        z_copy(k, 0).wait_send()
        z_copy(k, 1).wait_send()

    def drain(zz):
        x_copy(y, zz, 0).wait_send()
        x_copy(y, zz, 1).wait_send()
        for xx in range(2):
            c_copy(y, zz, xx, 0).wait_send()
            c_copy(y, zz, xx, 1).wait_send()

        def each(j):
            yy = ymod(j)
            x_copy(yy, zz, 1).wait_send()
            y_copy(j, zz, x, 1).wait_send()
            for xx in range(2):
                y_copy(j, zz, xx, 0).wait_send()
                c_copy(yy, zz, xx, 0).wait_send()
                c_copy(yy, zz, xx, 1).wait_send()

        y_range(each)

    z_range(0, drain)


def col_sum(v):
    size = v.shape[1]
    return v + pltpu.roll(v, 1, 1) + pltpu.roll(v, size - 1, 1)


def box(v):
    n = v.shape[0]
    return col_sum(v[0 : n - 2] + v[1 : n - 1] + v[2:n]) * (1.0 / 9.0)


def turn(v, step):
    if step == 1:
        return jnp.concatenate([v[:, -1:], v[:, :-1]], axis=1)
    return jnp.concatenate([v[:, 1:], v[:, :1]], axis=1)


def charbonnier(weight, delta):
    return weight * delta / jnp.sqrt(delta * delta + charb_sq)


def stencil(nblk, ncol, rows, cols, x_ref, y_ref, c_ref, flow_ref, gflow_ref, grad_ref):
    width = x_ref.shape[1]
    span = cols + SIDE
    i = lax.axis_index("blk")
    y = lax.axis_index("col")
    full_rows, full_cols = rows * nblk, cols * ncol

    def place(shape, row_axis, col_axis, first_row):
        r = lax.broadcasted_iota(jnp.int32, shape, row_axis) + (i * rows + first_row)
        w = lax.broadcasted_iota(jnp.int32, shape, col_axis)
        w = jnp.where(w >= cols + SIDE // 2, w - span, w) + y * cols
        return r, w

    def inside(shape, first_row):
        r, w = place(shape, 0, 1, first_row)
        return (r >= 0) & (r < full_rows) & (w >= 0) & (w < full_cols)

    xraw = x_ref[...].astype(jnp.float32).reshape(rows + 4, span, width)
    keep = inside(xraw.shape, -2)
    xv = jnp.where(keep, xraw, 0.0)
    yv = jnp.where(keep, y_ref[...].astype(jnp.float32).reshape(rows + 4, span, width), 0.0)
    mx, my = box(xv), box(yv)
    vx = box(xv * xv) - mx * mx
    vy = box(yv * yv) - my * my
    cv = box(xv * yv) - mx * my
    n1 = 2.0 * mx * my + ssim_one
    n2 = 2.0 * cv + ssim_two
    d1 = mx * mx + my * my + ssim_one
    d2 = vx + vy + ssim_two
    inv1 = 1.0 / d1
    inv2 = 1.0 / d2
    inv = inv1 * inv2
    ssim = n1 * n2 * inv
    a = ssim * my * inv1 - mx * n2 * inv
    b = 0.5 * ssim * inv2
    cc = -n1 * inv
    first = a - 2.0 * b * my - cc * mx
    ok = inside(mx.shape, -1)
    g1 = box(jnp.where(ok, first, 0.0))
    g2 = box(jnp.where(ok, b, 0.0))
    g3 = box(jnp.where(ok, cc, 0.0))
    yc = yv[2 : rows + 2]
    xc = xv[2 : rows + 2]
    grad_ref[...] = (g1 + 2.0 * yc * g2 + xc * g3)[:, 0:cols]

    sums = jnp.transpose(c_ref[...])

    def plane(n):
        line = sums[n : n + 1]
        return jnp.concatenate([line[:, r * span : (r + 1) * span] for r in range(rows + 4)], axis=0)

    rr, ww = place((rows + 4, span), 0, 1, -2)
    fy = (plane(1) + 0.5) * (2.0 / full_rows) - 1.0 - ((rr.astype(jnp.float32) + 0.5) * (2.0 / full_rows) - 1.0)
    px = plane(2) + plane(3) * float(cols)
    fx = (px + 0.5) * (2.0 / full_cols) - 1.0 - ((ww.astype(jnp.float32) + 0.5) * (2.0 / full_cols) - 1.0)
    flow_ref[0] = fy[2 : rows + 2, 0:cols]
    flow_ref[1] = fx[2 : rows + 2, 0:cols]

    w_y = jnp.exp(-jnp.mean(jnp.abs(xraw[2 : rows + 3] - xraw[1 : rows + 2]), axis=-1))
    mid = xraw[2 : rows + 2]
    w_x = jnp.exp(-jnp.mean(jnp.abs(mid - pltpu.roll(mid, 1, 1)), axis=-1))
    er, _ = place((rows + 1, span), 0, 1, -1)
    use_y = (er >= 0) & (er <= full_rows - 2)
    _, ew = place((rows, span), 0, 1, 0)
    use_x = (ew >= 1) & (ew <= full_cols - 1)
    for n, f in enumerate((fy, fx)):
        push_y = jnp.where(use_y, charbonnier(w_y, f[2 : rows + 3] - f[1 : rows + 2]), 0.0)
        fm = f[2 : rows + 2]
        push_x = jnp.where(use_x, charbonnier(w_x, fm - turn(fm, 1)), 0.0)
        out = push_y[0:rows] - push_y[1 : rows + 1] + push_x - turn(push_x, -1)
        gflow_ref[n] = out[:, 0:cols]


def body(nblk, ncol, feat1, feat2):
    rows, cols, width = feat1.shape
    nz = nblk // 4
    count = (rows + 4) * (cols + SIDE)
    vmem = pl.BlockSpec(memory_space=pltpu.VMEM)
    dma = pltpu.SemaphoreType.DMA
    bf = jnp.bfloat16
    edges = (
        pltpu.VMEM((2, cols, width), bf),
        pltpu.VMEM((2, cols, width), bf),
        pltpu.VMEM((rows + 4, 16, width), bf),
        pltpu.VMEM((rows + 4, 16, width), bf),
    )
    xq, warped, sums = pl.pallas_call(
        functools.partial(gather_attend, nblk, ncol),
        out_shape=(
            jax.ShapeDtypeStruct((count, width), bf),
            jax.ShapeDtypeStruct((count, width), bf),
            jax.ShapeDtypeStruct((count, 128), jnp.float32),
        ),
        in_specs=[vmem] * 2,
        out_specs=(vmem, vmem, vmem),
        scratch_shapes=[
            pltpu.VMEM((ncol, nblk, rows, cols, width), bf),
            edges,
            edges,
            (
                pltpu.VMEM((1, cols, 128), jnp.float32),
                pltpu.VMEM((1, cols, 128), jnp.float32),
                pltpu.VMEM((rows, SIDE, 128), jnp.float32),
                pltpu.VMEM((rows, SIDE, 128), jnp.float32),
            ),
            pltpu.VMEM((rows, cols, width), bf),
            pltpu.VMEM((rows, cols, 128), jnp.float32),
            pltpu.VMEM((rows * cols, width), bf),
            pltpu.VMEM((rows + 4, cols + SIDE, width), jnp.float32),
            pltpu.VMEM((rows + 4, cols + SIDE, 128), jnp.float32),
            pltpu.VMEM((rows * cols, 128), jnp.float32),
            pltpu.VMEM((rows * cols, width), jnp.float32),
            pltpu.VMEM((rows * cols, 128), jnp.float32),
            dma((ncol, nblk, 2)),
            dma((nz - 1, 2)),
            dma((2, ncol, nz)),
            dma((2, ncol - 1, nz, 2)),
            dma((ncol, nblk // 2, 2)),
            dma((20,)),
            dma((20,)),
        ],
        compiler_params=pltpu.CompilerParams(
            collective_id=0, has_side_effects=True, vmem_limit_bytes=48 * 1024 * 1024
        ),
    )(feat1, feat2)
    return pl.pallas_call(
        functools.partial(stencil, nblk, ncol, rows, cols),
        out_shape=(
            jax.ShapeDtypeStruct((2, rows, cols), jnp.float32),
            jax.ShapeDtypeStruct((2, rows, cols), jnp.float32),
            jax.ShapeDtypeStruct((rows, cols, width), jnp.float32),
        ),
        in_specs=[vmem] * 3,
        out_specs=(vmem, vmem, vmem),
        compiler_params=pltpu.CompilerParams(vmem_limit_bytes=40 * 1024 * 1024),
    )(xq, warped, sums)


def solution(mesh):
    placed = (P("blk", "col", None), P("blk", "col", None))
    return jax.shard_map(
        functools.partial(body, mesh.shape["blk"], mesh.shape["col"]),
        mesh=mesh,
        in_specs=placed,
        out_specs=(P(None, "blk", "col"), P(None, "blk", "col"), P("blk", "col", None)),
        check_vma=False,
    )
```

```python
import functools
import math

import jax
import jax.numpy as jnp
from jax import lax
from jax.experimental import pallas as pl
from jax.experimental.pallas import tpu as pltpu
from jax.sharding import PartitionSpec as P

ssim_one = 0.01
ssim_two = 0.03
charb_sq = 0.0001
SIDE = 8
MESH = pl.DeviceIdType.MESH


def gather_attend(
    nblk, ncol, f1, f2, x_out, y_out, c_out,
    keys, x_bufs, y_bufs, c_bufs, own_y, own_c, query, ext, ext_c, peak, acc, acc_c,
    recv, send_z, send_x, send_y, send_c, halo_send, halo_recv,
):
    rows, cols, width = f1.shape
    half_rows = rows // 2
    nz = nblk // 4
    i = lax.axis_index("blk")
    y = lax.axis_index("col")
    c = lax.rem(i, 2)
    x = lax.rem(i // 2, 2)
    z = i // 4

    def blk_of(zz, xx, cc):
        return (zz * 2 + xx) * 2 + cc

    def zmod(k):
        if nz & (nz - 1):
            return lax.rem(z + k, nz)
        found = 0
        for bit in range(nz.bit_length() - 1):
            step = 2**bit
            found = found + lax.rem(z // step + k // step, 2) * step
        return found

    def ymod(k):
        return lax.rem(y + k, ncol)

    other_x = (blk_of(z, 1 - x, c), y)
    sibling = (blk_of(z, x, 1 - c), y)
    up, down = lax.rem(i + nblk - 1, nblk), lax.rem(i + 1, nblk)
    west, east = ymod(ncol - 1), ymod(1)

    keys[y, i] = f2[...]

    around = [(up, y), (down, y), (i, west), (i, east), (up, west), (up, east), (down, west), (down, east)]
    peers = [(blk_of(zmod(k), x, c), y) for k in range(1, nz)]
    peers += [(i, ymod(k)) for k in range(1, ncol)]
    peers += [other_x, sibling] + around
    barrier = pltpu.get_barrier_semaphore()
    for peer in peers:
        pl.semaphore_signal(barrier, inc=1, device_id=peer, device_id_type=MESH)
    pl.semaphore_wait(barrier, len(peers))

    def copy(yy, b, half, dest, sem):
        part = keys.at[yy, b, pl.ds(half * half_rows, half_rows)]
        return pltpu.make_async_remote_copy(
            src_ref=part, dst_ref=part, send_sem=sem, recv_sem=recv.at[yy, b, half],
            device_id=dest, device_id_type=MESH,
        )

    def arrived(yy, b, half):
        copy(yy, b, half, sibling, send_c.at[yy, b // 2, half]).wait_recv()

    def z_copy(k, half):
        return copy(y, i, half, (blk_of(zmod(k), x, c), y), send_z.at[k - 1, half])

    def x_copy(yy, zz, half):
        return copy(yy, blk_of(zz, x, c), half, other_x, send_x.at[half, yy, zz])

    def y_copy(k, zz, xx, half):
        return copy(y, blk_of(zz, xx, c), half, (i, ymod(k)), send_y.at[half, k - 1, zz, xx])

    def c_copy(yy, zz, xx, half):
        return copy(yy, blk_of(zz, xx, c), half, sibling, send_c.at[yy, zz * 2 + xx, half])

    def y_range(fn):
        if ncol == 2:
            fn(1)
        else:
            lax.fori_loop(1, ncol, lambda k, u: (fn(k), u)[1], 0)

    def z_range(low, fn):
        lax.fori_loop(low, nz, lambda k, u: (fn(k), u)[1], 0)

    def start_column(zz):
        x_copy(y, zz, 0).start()
        y_range(lambda k: y_copy(k, zz, x, 1).start())
        x_copy(y, zz, 1).start()
        y_range(lambda k: y_copy(k, zz, x, 0).start())
        c_copy(y, zz, x, 0).start()
        c_copy(y, zz, x, 1).start()

    def halo(src, dst, dest, n):
        return pltpu.make_async_remote_copy(
            src_ref=src, dst_ref=dst, send_sem=halo_send.at[n], recv_sem=halo_recv.at[n],
            device_id=dest, device_id_type=MESH,
        )

    first, last = pl.ds(0, 2), pl.ds(rows - 2, 2)
    lead, tail = pl.ds(0, 16), pl.ds(cols - 16, 16)
    mid, end = pl.ds(2, rows), pl.ds(rows + 2, 2)
    def eight(src, bufs, at):
        top_h, bot_h, left_h, right_h = bufs
        return [
            halo(src.at[last], top_h, (down, y), at),
            halo(src.at[first], bot_h, (up, y), at + 1),
            halo(src.at[:, tail], left_h.at[mid], (i, east), at + 2),
            halo(src.at[:, lead], right_h.at[mid], (i, west), at + 3),
            halo(src.at[last, tail], left_h.at[first], (down, east), at + 4),
            halo(src.at[last, lead], right_h.at[first], (down, west), at + 5),
            halo(src.at[first, tail], left_h.at[end], (up, east), at + 6),
            halo(src.at[first, lead], right_h.at[end], (up, west), at + 7),
        ]

    halos = eight(f1, x_bufs, 0)
    late = [
        halo(own_c.at[pl.ds(rows - 1, 1)], c_bufs[0], (down, y), 16),
        halo(own_c.at[pl.ds(0, 1)], c_bufs[1], (up, y), 17),
        halo(own_c.at[:, pl.ds(cols - SIDE, SIDE)], c_bufs[2], (i, east), 18),
        halo(own_c.at[:, pl.ds(0, SIDE)], c_bufs[3], (i, west), 19),
    ] + eight(own_y, y_bufs, 8)

    for k in range(1, nz):
        z_copy(k, 0).start()
        z_copy(k, 1).start()
    for item in halos:
        item.start()
    start_column(z)

    peak[...] = jnp.full_like(peak, -1e30)
    acc[...] = jnp.zeros_like(acc)
    acc_c[...] = jnp.zeros_like(acc_c)
    per = 2 * rows * cols
    where = lax.broadcasted_iota(jnp.int32, (2 * rows, cols, 128), 0)
    along = lax.broadcasted_iota(jnp.int32, (2 * rows, cols, 128), 1)
    lane = lax.broadcasted_iota(jnp.int32, (2 * rows, cols, 128), 2)
    pattern = jnp.where(lane == 0, 1, jnp.where(lane == 1, where, jnp.where(lane == 2, along, 0)))
    pattern = pattern.astype(jnp.float32).reshape(per, 128)
    lane_row = lax.broadcasted_iota(jnp.int32, (1, 128), 1)

    count = (rows + 4) * (cols + SIDE)
    scale = 1.0 / math.sqrt(width)
    query[...] = (f1[...].astype(jnp.float32) * scale).reshape(rows * cols, width).astype(jnp.bfloat16)

    def widen(own, bufs):
        top_h, bot_h, left_h, right_h = bufs
        ext[0:2, 0:cols] = top_h[...].astype(jnp.float32)
        ext[2 : rows + 2, 0:cols] = own[...].astype(jnp.float32)
        ext[rows + 2 : rows + 4, 0:cols] = bot_h[...].astype(jnp.float32)
        spot = lax.broadcasted_iota(jnp.int32, (rows + 4, SIDE, width), 1)
        ext[:, cols : cols + SIDE] = jnp.where(
            spot < SIDE // 2,
            right_h[...].astype(jnp.float32)[:, 0:SIDE],
            left_h[...].astype(jnp.float32)[:, 16 - SIDE : 16],
        )
        return ext[...].reshape(count, width).astype(jnp.bfloat16)

    def absorb(*chips):
        blocks, coords, scores = [], [], []
        for yy, zz, xx in chips:
            chip = zz * 2 + xx
            for half in range(2):
                arrived(yy, chip * 2 + 1 - c, half)
            block = keys[yy, pl.ds(chip * 2, 2)].reshape(per, width)
            base = jnp.where(lane_row == 1, chip * 2 * rows, jnp.where(lane_row == 3, yy, 0))
            blocks.append(block)
            coords.append((pattern + base.astype(jnp.float32)).astype(jnp.bfloat16))
            scores.append(
                lax.dot_general(
                    query[...], block, (((1,), (1,)), ((), ())), preferred_element_type=jnp.float32
                )
            )
        old = peak[...]
        new = old
        for score in scores:
            new = jnp.maximum(new, jnp.max(score, axis=1, keepdims=True))
        peak[...] = new
        shrink = jnp.exp(old - new)
        mixed = acc[...] * shrink[:, 0:1]
        placed = acc_c[...] * shrink
        for block, coord, score in zip(blocks, coords, scores):
            full = jnp.exp(score - new[:, 0:1])
            expo = full.astype(jnp.bfloat16)
            rest = (full - expo.astype(jnp.float32)).astype(jnp.bfloat16)
            mixed = mixed + jnp.dot(expo, block, preferred_element_type=jnp.float32)
            placed = placed + jnp.dot(expo, coord, preferred_element_type=jnp.float32)
            placed = placed + jnp.dot(rest, coord, preferred_element_type=jnp.float32)
        acc[...] = mixed
        acc_c[...] = placed

    def absorb_two(zz):
        if ncol == 2:
            absorb((y, zz, 1 - x), (1 - y, zz, x))
        else:
            absorb((y, zz, 1 - x))
            y_range(lambda j: absorb((ymod(j), zz, x)))

    absorb((y, z, x))

    def wave_z(k):
        zz = zmod(k)
        arrived(y, blk_of(zz, x, c), 0)
        arrived(y, blk_of(zz, x, c), 1)
        start_column(zz)

    z_range(1, wave_z)

    def wave_one(k):
        zz = zmod(k)
        arrived(y, blk_of(zz, 1 - x, c), 0)
        y_range(lambda j: y_copy(j, zz, 1 - x, 0).start())
        c_copy(y, zz, 1 - x, 0).start()

        def take(j):
            yy = ymod(j)
            arrived(yy, blk_of(zz, x, c), 1)
            x_copy(yy, zz, 1).start()
            c_copy(yy, zz, x, 1).start()

        y_range(take)

    z_range(0, wave_one)

    def wave_two(k):
        zz = zmod(k)
        arrived(y, blk_of(zz, 1 - x, c), 1)
        c_copy(y, zz, 1 - x, 1).start()

        def take(j):
            yy = ymod(j)
            arrived(yy, blk_of(zz, x, c), 0)
            c_copy(yy, zz, x, 0).start()

        y_range(take)

        @pl.when(k > 0)
        def _():
            absorb((y, zz, x))
            absorb_two(zmod(k - 1))

    z_range(0, wave_two)

    def wave_three(k):
        zz = zmod(k)

        def take(j):
            yy = ymod(j)
            arrived(yy, blk_of(zz, 1 - x, c), 0)
            c_copy(yy, zz, 1 - x, 0).start()
            arrived(yy, blk_of(zz, 1 - x, c), 1)
            c_copy(yy, zz, 1 - x, 1).start()

        y_range(take)

        @pl.when(k == 0)
        def _():
            absorb_two(zmod(nz - 1))

        @pl.when(k > 0)
        def _():
            y_range(lambda j: absorb((ymod(j), zmod(k - 1), 1 - x)))

    z_range(0, wave_three)
    y_range(lambda j: absorb((ymod(j), zmod(nz - 1), 1 - x)))

    total = acc_c[:, 0:1]
    own_c[...] = (acc_c[...] / total).reshape(rows, cols, 128)
    own_y[...] = (acc[...] / total).reshape(rows, cols, width).astype(jnp.bfloat16)
    for item in late:
        item.start()
    for item in halos:
        item.wait_recv()
    x_out[...] = widen(f1, x_bufs)
    ext_c[...] = jnp.zeros_like(ext_c)
    ext_c[2 : rows + 2, 0:cols] = own_c[...]
    for item in late:
        item.wait_recv()
    ext_c[1:2, 0:cols] = c_bufs[0][...]
    ext_c[rows + 2 : rows + 3, 0:cols] = c_bufs[1][...]
    spot_c = lax.broadcasted_iota(jnp.int32, (rows, SIDE, 128), 1)
    ext_c[2 : rows + 2, cols : cols + SIDE] = jnp.where(
        spot_c < SIDE // 2, c_bufs[3][...], c_bufs[2][...]
    )
    c_out[...] = ext_c[...].reshape(count, 128)
    y_out[...] = widen(own_y, y_bufs)

    for item in late:
        item.wait_send()
    for item in halos:
        item.wait_send()
    for k in range(1, nz):
        z_copy(k, 0).wait_send()
        z_copy(k, 1).wait_send()

    def drain(zz):
        x_copy(y, zz, 0).wait_send()
        x_copy(y, zz, 1).wait_send()
        for xx in range(2):
            c_copy(y, zz, xx, 0).wait_send()
            c_copy(y, zz, xx, 1).wait_send()

        def each(j):
            yy = ymod(j)
            x_copy(yy, zz, 1).wait_send()
            y_copy(j, zz, x, 1).wait_send()
            for xx in range(2):
                y_copy(j, zz, xx, 0).wait_send()
                c_copy(yy, zz, xx, 0).wait_send()
                c_copy(yy, zz, xx, 1).wait_send()

        y_range(each)

    z_range(0, drain)


def col_sum(v):
    size = v.shape[1]
    return v + pltpu.roll(v, 1, 1) + pltpu.roll(v, size - 1, 1)


def box(v):
    n = v.shape[0]
    return col_sum(v[0 : n - 2] + v[1 : n - 1] + v[2:n]) * (1.0 / 9.0)


def turn(v, step):
    if step == 1:
        return jnp.concatenate([v[:, -1:], v[:, :-1]], axis=1)
    return jnp.concatenate([v[:, 1:], v[:, :1]], axis=1)


def charbonnier(weight, delta):
    return weight * delta / jnp.sqrt(delta * delta + charb_sq)


def stencil(nblk, ncol, rows, cols, x_ref, y_ref, c_ref, flow_ref, gflow_ref, grad_ref):
    width = x_ref.shape[1]
    span = cols + SIDE
    i = lax.axis_index("blk")
    y = lax.axis_index("col")
    full_rows, full_cols = rows * nblk, cols * ncol

    def place(shape, row_axis, col_axis, first_row):
        r = lax.broadcasted_iota(jnp.int32, shape, row_axis) + (i * rows + first_row)
        w = lax.broadcasted_iota(jnp.int32, shape, col_axis)
        w = jnp.where(w >= cols + SIDE // 2, w - span, w) + y * cols
        return r, w

    def inside(shape, first_row):
        r, w = place(shape, 0, 1, first_row)
        return (r >= 0) & (r < full_rows) & (w >= 0) & (w < full_cols)

    xraw = x_ref[...].astype(jnp.float32).reshape(rows + 4, span, width)
    keep = inside(xraw.shape, -2)
    xv = jnp.where(keep, xraw, 0.0)
    yv = jnp.where(keep, y_ref[...].astype(jnp.float32).reshape(rows + 4, span, width), 0.0)
    mx, my = box(xv), box(yv)
    vx = box(xv * xv) - mx * mx
    vy = box(yv * yv) - my * my
    cv = box(xv * yv) - mx * my
    n1 = 2.0 * mx * my + ssim_one
    n2 = 2.0 * cv + ssim_two
    d1 = mx * mx + my * my + ssim_one
    d2 = vx + vy + ssim_two
    inv1 = 1.0 / d1
    inv2 = 1.0 / d2
    inv = inv1 * inv2
    ssim = n1 * n2 * inv
    a = ssim * my * inv1 - mx * n2 * inv
    b = 0.5 * ssim * inv2
    cc = -n1 * inv
    first = a - 2.0 * b * my - cc * mx
    ok = inside(mx.shape, -1)
    g1 = box(jnp.where(ok, first, 0.0))
    g2 = box(jnp.where(ok, b, 0.0))
    g3 = box(jnp.where(ok, cc, 0.0))
    yc = yv[2 : rows + 2]
    xc = xv[2 : rows + 2]
    grad_ref[...] = (g1 + 2.0 * yc * g2 + xc * g3)[:, 0:cols]

    sums = jnp.transpose(c_ref[...])

    def plane(n):
        line = sums[n : n + 1]
        return jnp.concatenate([line[:, r * span : (r + 1) * span] for r in range(rows + 4)], axis=0)

    rr, ww = place((rows + 4, span), 0, 1, -2)
    fy = (plane(1) + 0.5) * (2.0 / full_rows) - 1.0 - ((rr.astype(jnp.float32) + 0.5) * (2.0 / full_rows) - 1.0)
    px = plane(2) + plane(3) * float(cols)
    fx = (px + 0.5) * (2.0 / full_cols) - 1.0 - ((ww.astype(jnp.float32) + 0.5) * (2.0 / full_cols) - 1.0)
    flow_ref[0] = fy[2 : rows + 2, 0:cols]
    flow_ref[1] = fx[2 : rows + 2, 0:cols]

    w_y = jnp.exp(-jnp.mean(jnp.abs(xraw[2 : rows + 3] - xraw[1 : rows + 2]), axis=-1))
    mid = xraw[2 : rows + 2]
    w_x = jnp.exp(-jnp.mean(jnp.abs(mid - pltpu.roll(mid, 1, 1)), axis=-1))
    er, _ = place((rows + 1, span), 0, 1, -1)
    use_y = (er >= 0) & (er <= full_rows - 2)
    _, ew = place((rows, span), 0, 1, 0)
    use_x = (ew >= 1) & (ew <= full_cols - 1)
    for n, f in enumerate((fy, fx)):
        push_y = jnp.where(use_y, charbonnier(w_y, f[2 : rows + 3] - f[1 : rows + 2]), 0.0)
        fm = f[2 : rows + 2]
        push_x = jnp.where(use_x, charbonnier(w_x, fm - turn(fm, 1)), 0.0)
        out = push_y[0:rows] - push_y[1 : rows + 1] + push_x - turn(push_x, -1)
        gflow_ref[n] = out[:, 0:cols]


def body(nblk, ncol, feat1, feat2):
    rows, cols, width = feat1.shape
    nz = nblk // 4
    count = (rows + 4) * (cols + SIDE)
    vmem = pl.BlockSpec(memory_space=pltpu.VMEM)
    dma = pltpu.SemaphoreType.DMA
    bf = jnp.bfloat16
    edges = (
        pltpu.VMEM((2, cols, width), bf),
        pltpu.VMEM((2, cols, width), bf),
        pltpu.VMEM((rows + 4, 16, width), bf),
        pltpu.VMEM((rows + 4, 16, width), bf),
    )
    xq, warped, sums = pl.pallas_call(
        functools.partial(gather_attend, nblk, ncol),
        out_shape=(
            jax.ShapeDtypeStruct((count, width), bf),
            jax.ShapeDtypeStruct((count, width), bf),
            jax.ShapeDtypeStruct((count, 128), jnp.float32),
        ),
        in_specs=[vmem] * 2,
        out_specs=(vmem, vmem, vmem),
        scratch_shapes=[
            pltpu.VMEM((ncol, nblk, rows, cols, width), bf),
            edges,
            edges,
            (
                pltpu.VMEM((1, cols, 128), jnp.float32),
                pltpu.VMEM((1, cols, 128), jnp.float32),
                pltpu.VMEM((rows, SIDE, 128), jnp.float32),
                pltpu.VMEM((rows, SIDE, 128), jnp.float32),
            ),
            pltpu.VMEM((rows, cols, width), bf),
            pltpu.VMEM((rows, cols, 128), jnp.float32),
            pltpu.VMEM((rows * cols, width), bf),
            pltpu.VMEM((rows + 4, cols + SIDE, width), jnp.float32),
            pltpu.VMEM((rows + 4, cols + SIDE, 128), jnp.float32),
            pltpu.VMEM((rows * cols, 128), jnp.float32),
            pltpu.VMEM((rows * cols, width), jnp.float32),
            pltpu.VMEM((rows * cols, 128), jnp.float32),
            dma((ncol, nblk, 2)),
            dma((nz - 1, 2)),
            dma((2, ncol, nz)),
            dma((2, ncol - 1, nz, 2)),
            dma((ncol, nblk // 2, 2)),
            dma((20,)),
            dma((20,)),
        ],
        compiler_params=pltpu.CompilerParams(
            collective_id=0, has_side_effects=True, vmem_limit_bytes=48 * 1024 * 1024
        ),
    )(feat1, feat2)
    return pl.pallas_call(
        functools.partial(stencil, nblk, ncol, rows, cols),
        out_shape=(
            jax.ShapeDtypeStruct((2, rows, cols), jnp.float32),
            jax.ShapeDtypeStruct((2, rows, cols), jnp.float32),
            jax.ShapeDtypeStruct((rows, cols, width), jnp.float32),
        ),
        in_specs=[vmem] * 3,
        out_specs=(vmem, vmem, vmem),
        compiler_params=pltpu.CompilerParams(vmem_limit_bytes=40 * 1024 * 1024),
    )(xq, warped, sums)


def solution(mesh):
    placed = (P("blk", "col", None), P("blk", "col", None))
    return jax.shard_map(
        functools.partial(body, mesh.shape["blk"], mesh.shape["col"]),
        mesh=mesh,
        in_specs=placed,
        out_specs=(P(None, "blk", "col"), P(None, "blk", "col"), P("blk", "col", None)),
        check_vma=False,
    )
```

```python
import functools
import math

import jax
import jax.numpy as jnp
from jax import lax
from jax.experimental import pallas as pl
from jax.experimental.pallas import tpu as pltpu
from jax.sharding import PartitionSpec as P

ssim_one = 0.01
ssim_two = 0.03
charb_sq = 0.0001
SIDE = 8
MESH = pl.DeviceIdType.MESH


def gather_attend(
    nblk, ncol, f1, f2, x_out, y_out, c_out,
    keys, x_bufs, y_bufs, c_bufs, own_y, own_c, query, ext, ext_c, peak, acc, acc_c,
    recv, send_z, send_x, send_y, send_c, halo_send, halo_recv,
):
    rows, cols, width = f1.shape
    half_rows = rows // 2
    nz = nblk // 4
    i = lax.axis_index("blk")
    y = lax.axis_index("col")
    c = lax.rem(i, 2)
    x = lax.rem(i // 2, 2)
    z = i // 4

    def blk_of(zz, xx, cc):
        return (zz * 2 + xx) * 2 + cc

    def zmod(k):
        if nz & (nz - 1):
            return lax.rem(z + k, nz)
        found = 0
        for bit in range(nz.bit_length() - 1):
            step = 2**bit
            found = found + lax.rem(z // step + k // step, 2) * step
        return found

    def ymod(k):
        return lax.rem(y + k, ncol)

    other_x = (blk_of(z, 1 - x, c), y)
    sibling = (blk_of(z, x, 1 - c), y)
    up, down = lax.rem(i + nblk - 1, nblk), lax.rem(i + 1, nblk)
    west, east = ymod(ncol - 1), ymod(1)

    keys[y, i] = f2[...]

    around = [(up, y), (down, y), (i, west), (i, east), (up, west), (up, east), (down, west), (down, east)]
    peers = [(blk_of(zmod(k), x, c), y) for k in range(1, nz)]
    peers += [(i, ymod(k)) for k in range(1, ncol)]
    peers += [other_x, sibling] + around
    barrier = pltpu.get_barrier_semaphore()
    for peer in peers:
        pl.semaphore_signal(barrier, inc=1, device_id=peer, device_id_type=MESH)
    pl.semaphore_wait(barrier, len(peers))

    def copy(yy, b, half, dest, sem):
        part = keys.at[yy, b, pl.ds(half * half_rows, half_rows)]
        return pltpu.make_async_remote_copy(
            src_ref=part, dst_ref=part, send_sem=sem, recv_sem=recv.at[yy, b, half],
            device_id=dest, device_id_type=MESH,
        )

    def arrived(yy, b, half):
        copy(yy, b, half, sibling, send_c.at[yy, b // 2, half]).wait_recv()

    def z_copy(k, half):
        return copy(y, i, half, (blk_of(zmod(k), x, c), y), send_z.at[k - 1, half])

    def x_copy(yy, zz, half):
        return copy(yy, blk_of(zz, x, c), half, other_x, send_x.at[half, yy, zz])

    def y_copy(k, zz, xx, half):
        return copy(y, blk_of(zz, xx, c), half, (i, ymod(k)), send_y.at[half, k - 1, zz, xx])

    def c_copy(yy, zz, xx, half):
        return copy(yy, blk_of(zz, xx, c), half, sibling, send_c.at[yy, zz * 2 + xx, half])

    def y_range(fn):
        if ncol == 2:
            fn(1)
        else:
            lax.fori_loop(1, ncol, lambda k, u: (fn(k), u)[1], 0)

    def z_range(low, fn):
        lax.fori_loop(low, nz, lambda k, u: (fn(k), u)[1], 0)

    def start_column(zz):
        x_copy(y, zz, 0).start()
        y_range(lambda k: y_copy(k, zz, x, 1).start())
        x_copy(y, zz, 1).start()
        y_range(lambda k: y_copy(k, zz, x, 0).start())
        c_copy(y, zz, x, 0).start()
        c_copy(y, zz, x, 1).start()

    def halo(src, dst, dest, n):
        return pltpu.make_async_remote_copy(
            src_ref=src, dst_ref=dst, send_sem=halo_send.at[n], recv_sem=halo_recv.at[n],
            device_id=dest, device_id_type=MESH,
        )

    first, last = pl.ds(0, 2), pl.ds(rows - 2, 2)
    lead, tail = pl.ds(0, 16), pl.ds(cols - 16, 16)
    mid, end = pl.ds(2, rows), pl.ds(rows + 2, 2)
    def eight(src, bufs, at):
        top_h, bot_h, left_h, right_h = bufs
        return [
            halo(src.at[last], top_h, (down, y), at),
            halo(src.at[first], bot_h, (up, y), at + 1),
            halo(src.at[:, tail], left_h.at[mid], (i, east), at + 2),
            halo(src.at[:, lead], right_h.at[mid], (i, west), at + 3),
            halo(src.at[last, tail], left_h.at[first], (down, east), at + 4),
            halo(src.at[last, lead], right_h.at[first], (down, west), at + 5),
            halo(src.at[first, tail], left_h.at[end], (up, east), at + 6),
            halo(src.at[first, lead], right_h.at[end], (up, west), at + 7),
        ]

    halos = eight(f1, x_bufs, 0)
    late = [
        halo(own_c.at[pl.ds(rows - 1, 1)], c_bufs[0], (down, y), 16),
        halo(own_c.at[pl.ds(0, 1)], c_bufs[1], (up, y), 17),
        halo(own_c.at[:, pl.ds(cols - SIDE, SIDE)], c_bufs[2], (i, east), 18),
        halo(own_c.at[:, pl.ds(0, SIDE)], c_bufs[3], (i, west), 19),
    ] + eight(own_y, y_bufs, 8)

    for k in range(1, nz):
        z_copy(k, 0).start()
        z_copy(k, 1).start()
    start_column(z)

    peak[...] = jnp.full_like(peak, -1e30)
    acc[...] = jnp.zeros_like(acc)
    acc_c[...] = jnp.zeros_like(acc_c)
    per = 2 * rows * cols
    where = lax.broadcasted_iota(jnp.int32, (2 * rows, cols, 128), 0)
    along = lax.broadcasted_iota(jnp.int32, (2 * rows, cols, 128), 1)
    lane = lax.broadcasted_iota(jnp.int32, (2 * rows, cols, 128), 2)
    pattern = jnp.where(lane == 0, 1, jnp.where(lane == 1, where, jnp.where(lane == 2, along, 0)))
    pattern = pattern.astype(jnp.float32).reshape(per, 128)
    lane_row = lax.broadcasted_iota(jnp.int32, (1, 128), 1)

    count = (rows + 4) * (cols + SIDE)
    scale = 1.0 / math.sqrt(width)
    query[...] = (f1[...].astype(jnp.float32) * scale).reshape(rows * cols, width).astype(jnp.bfloat16)

    def widen(own, bufs):
        top_h, bot_h, left_h, right_h = bufs
        ext[0:2, 0:cols] = top_h[...].astype(jnp.float32)
        ext[2 : rows + 2, 0:cols] = own[...].astype(jnp.float32)
        ext[rows + 2 : rows + 4, 0:cols] = bot_h[...].astype(jnp.float32)
        spot = lax.broadcasted_iota(jnp.int32, (rows + 4, SIDE, width), 1)
        ext[:, cols : cols + SIDE] = jnp.where(
            spot < SIDE // 2,
            right_h[...].astype(jnp.float32)[:, 0:SIDE],
            left_h[...].astype(jnp.float32)[:, 16 - SIDE : 16],
        )
        return ext[...].reshape(count, width).astype(jnp.bfloat16)

    def absorb(*chips):
        blocks, coords, scores = [], [], []
        for yy, zz, xx in chips:
            chip = zz * 2 + xx
            for half in range(2):
                arrived(yy, chip * 2 + 1 - c, half)
            block = keys[yy, pl.ds(chip * 2, 2)].reshape(per, width)
            base = jnp.where(lane_row == 1, chip * 2 * rows, jnp.where(lane_row == 3, yy, 0))
            blocks.append(block)
            coords.append((pattern + base.astype(jnp.float32)).astype(jnp.bfloat16))
            scores.append(
                lax.dot_general(
                    query[...], block, (((1,), (1,)), ((), ())), preferred_element_type=jnp.float32
                )
            )
        old = peak[...]
        new = old
        for score in scores:
            new = jnp.maximum(new, jnp.max(score, axis=1, keepdims=True))
        peak[...] = new
        shrink = jnp.exp(old - new)
        mixed = acc[...] * shrink[:, 0:1]
        placed = acc_c[...] * shrink
        for block, coord, score in zip(blocks, coords, scores):
            full = jnp.exp(score - new[:, 0:1])
            expo = full.astype(jnp.bfloat16)
            rest = (full - expo.astype(jnp.float32)).astype(jnp.bfloat16)
            mixed = mixed + jnp.dot(expo, block, preferred_element_type=jnp.float32)
            placed = placed + jnp.dot(expo, coord, preferred_element_type=jnp.float32)
            placed = placed + jnp.dot(rest, coord, preferred_element_type=jnp.float32)
        acc[...] = mixed
        acc_c[...] = placed

    def absorb_two(zz):
        if ncol == 2:
            absorb((y, zz, 1 - x), (1 - y, zz, x))
        else:
            absorb((y, zz, 1 - x))
            y_range(lambda j: absorb((ymod(j), zz, x)))

    absorb((y, z, x))

    def wave_z(k):
        zz = zmod(k)
        arrived(y, blk_of(zz, x, c), 0)
        arrived(y, blk_of(zz, x, c), 1)
        start_column(zz)

    z_range(1, wave_z)
    for item in halos:
        item.start()

    def wave_one(k):
        zz = zmod(k)
        arrived(y, blk_of(zz, 1 - x, c), 0)
        y_range(lambda j: y_copy(j, zz, 1 - x, 0).start())
        c_copy(y, zz, 1 - x, 0).start()

        def take(j):
            yy = ymod(j)
            arrived(yy, blk_of(zz, x, c), 1)
            x_copy(yy, zz, 1).start()
            c_copy(yy, zz, x, 1).start()

        y_range(take)

        @pl.when(k > 0)
        def _():
            absorb((y, zz, x))

    z_range(0, wave_one)

    def wave_two(k):
        zz = zmod(k)
        arrived(y, blk_of(zz, 1 - x, c), 1)
        c_copy(y, zz, 1 - x, 1).start()

        def take(j):
            yy = ymod(j)
            arrived(yy, blk_of(zz, x, c), 0)
            c_copy(yy, zz, x, 0).start()

        y_range(take)

        @pl.when(k > 0)
        def _():
            absorb_two(zmod(k - 1))

    z_range(0, wave_two)

    def wave_three(k):
        zz = zmod(k)

        def take(j):
            yy = ymod(j)
            arrived(yy, blk_of(zz, 1 - x, c), 0)
            c_copy(yy, zz, 1 - x, 0).start()
            arrived(yy, blk_of(zz, 1 - x, c), 1)
            c_copy(yy, zz, 1 - x, 1).start()

        y_range(take)

        @pl.when(k == 0)
        def _():
            absorb_two(zmod(nz - 1))

        @pl.when(k > 0)
        def _():
            y_range(lambda j: absorb((ymod(j), zmod(k - 1), 1 - x)))

    z_range(0, wave_three)
    y_range(lambda j: absorb((ymod(j), zmod(nz - 1), 1 - x)))

    total = acc_c[:, 0:1]
    own_c[...] = (acc_c[...] / total).reshape(rows, cols, 128)
    own_y[...] = (acc[...] / total).reshape(rows, cols, width).astype(jnp.bfloat16)
    for item in late:
        item.start()
    for item in halos:
        item.wait_recv()
    x_out[...] = widen(f1, x_bufs)
    ext_c[...] = jnp.zeros_like(ext_c)
    ext_c[2 : rows + 2, 0:cols] = own_c[...]
    for item in late:
        item.wait_recv()
    ext_c[1:2, 0:cols] = c_bufs[0][...]
    ext_c[rows + 2 : rows + 3, 0:cols] = c_bufs[1][...]
    spot_c = lax.broadcasted_iota(jnp.int32, (rows, SIDE, 128), 1)
    ext_c[2 : rows + 2, cols : cols + SIDE] = jnp.where(
        spot_c < SIDE // 2, c_bufs[3][...], c_bufs[2][...]
    )
    c_out[...] = ext_c[...].reshape(count, 128)
    y_out[...] = widen(own_y, y_bufs)

    for item in late:
        item.wait_send()
    for item in halos:
        item.wait_send()
    for k in range(1, nz):
        z_copy(k, 0).wait_send()
        z_copy(k, 1).wait_send()

    def drain(zz):
        x_copy(y, zz, 0).wait_send()
        x_copy(y, zz, 1).wait_send()
        for xx in range(2):
            c_copy(y, zz, xx, 0).wait_send()
            c_copy(y, zz, xx, 1).wait_send()

        def each(j):
            yy = ymod(j)
            x_copy(yy, zz, 1).wait_send()
            y_copy(j, zz, x, 1).wait_send()
            for xx in range(2):
                y_copy(j, zz, xx, 0).wait_send()
                c_copy(yy, zz, xx, 0).wait_send()
                c_copy(yy, zz, xx, 1).wait_send()

        y_range(each)

    z_range(0, drain)


def col_sum(v):
    size = v.shape[1]
    return v + pltpu.roll(v, 1, 1) + pltpu.roll(v, size - 1, 1)


def box(v):
    n = v.shape[0]
    return col_sum(v[0 : n - 2] + v[1 : n - 1] + v[2:n]) * (1.0 / 9.0)


def turn(v, step):
    if step == 1:
        return jnp.concatenate([v[:, -1:], v[:, :-1]], axis=1)
    return jnp.concatenate([v[:, 1:], v[:, :1]], axis=1)


def charbonnier(weight, delta):
    return weight * delta / jnp.sqrt(delta * delta + charb_sq)


def stencil(nblk, ncol, rows, cols, x_ref, y_ref, c_ref, flow_ref, gflow_ref, grad_ref):
    width = x_ref.shape[1]
    span = cols + SIDE
    i = lax.axis_index("blk")
    y = lax.axis_index("col")
    full_rows, full_cols = rows * nblk, cols * ncol

    def place(shape, row_axis, col_axis, first_row):
        r = lax.broadcasted_iota(jnp.int32, shape, row_axis) + (i * rows + first_row)
        w = lax.broadcasted_iota(jnp.int32, shape, col_axis)
        w = jnp.where(w >= cols + SIDE // 2, w - span, w) + y * cols
        return r, w

    def inside(shape, first_row):
        r, w = place(shape, 0, 1, first_row)
        return (r >= 0) & (r < full_rows) & (w >= 0) & (w < full_cols)

    xraw = x_ref[...].astype(jnp.float32).reshape(rows + 4, span, width)
    keep = inside(xraw.shape, -2)
    xv = jnp.where(keep, xraw, 0.0)
    yv = jnp.where(keep, y_ref[...].astype(jnp.float32).reshape(rows + 4, span, width), 0.0)
    mx, my = box(xv), box(yv)
    vx = box(xv * xv) - mx * mx
    vy = box(yv * yv) - my * my
    cv = box(xv * yv) - mx * my
    n1 = 2.0 * mx * my + ssim_one
    n2 = 2.0 * cv + ssim_two
    d1 = mx * mx + my * my + ssim_one
    d2 = vx + vy + ssim_two
    inv1 = 1.0 / d1
    inv2 = 1.0 / d2
    inv = inv1 * inv2
    ssim = n1 * n2 * inv
    a = ssim * my * inv1 - mx * n2 * inv
    b = 0.5 * ssim * inv2
    cc = -n1 * inv
    first = a - 2.0 * b * my - cc * mx
    ok = inside(mx.shape, -1)
    g1 = box(jnp.where(ok, first, 0.0))
    g2 = box(jnp.where(ok, b, 0.0))
    g3 = box(jnp.where(ok, cc, 0.0))
    yc = yv[2 : rows + 2]
    xc = xv[2 : rows + 2]
    grad_ref[...] = (g1 + 2.0 * yc * g2 + xc * g3)[:, 0:cols]

    sums = jnp.transpose(c_ref[...])

    def plane(n):
        line = sums[n : n + 1]
        return jnp.concatenate([line[:, r * span : (r + 1) * span] for r in range(rows + 4)], axis=0)

    rr, ww = place((rows + 4, span), 0, 1, -2)
    fy = (plane(1) + 0.5) * (2.0 / full_rows) - 1.0 - ((rr.astype(jnp.float32) + 0.5) * (2.0 / full_rows) - 1.0)
    px = plane(2) + plane(3) * float(cols)
    fx = (px + 0.5) * (2.0 / full_cols) - 1.0 - ((ww.astype(jnp.float32) + 0.5) * (2.0 / full_cols) - 1.0)
    flow_ref[0] = fy[2 : rows + 2, 0:cols]
    flow_ref[1] = fx[2 : rows + 2, 0:cols]

    w_y = jnp.exp(-jnp.mean(jnp.abs(xraw[2 : rows + 3] - xraw[1 : rows + 2]), axis=-1))
    mid = xraw[2 : rows + 2]
    w_x = jnp.exp(-jnp.mean(jnp.abs(mid - pltpu.roll(mid, 1, 1)), axis=-1))
    er, _ = place((rows + 1, span), 0, 1, -1)
    use_y = (er >= 0) & (er <= full_rows - 2)
    _, ew = place((rows, span), 0, 1, 0)
    use_x = (ew >= 1) & (ew <= full_cols - 1)
    for n, f in enumerate((fy, fx)):
        push_y = jnp.where(use_y, charbonnier(w_y, f[2 : rows + 3] - f[1 : rows + 2]), 0.0)
        fm = f[2 : rows + 2]
        push_x = jnp.where(use_x, charbonnier(w_x, fm - turn(fm, 1)), 0.0)
        out = push_y[0:rows] - push_y[1 : rows + 1] + push_x - turn(push_x, -1)
        gflow_ref[n] = out[:, 0:cols]


def body(nblk, ncol, feat1, feat2):
    rows, cols, width = feat1.shape
    nz = nblk // 4
    count = (rows + 4) * (cols + SIDE)
    vmem = pl.BlockSpec(memory_space=pltpu.VMEM)
    dma = pltpu.SemaphoreType.DMA
    bf = jnp.bfloat16
    edges = (
        pltpu.VMEM((2, cols, width), bf),
        pltpu.VMEM((2, cols, width), bf),
        pltpu.VMEM((rows + 4, 16, width), bf),
        pltpu.VMEM((rows + 4, 16, width), bf),
    )
    xq, warped, sums = pl.pallas_call(
        functools.partial(gather_attend, nblk, ncol),
        out_shape=(
            jax.ShapeDtypeStruct((count, width), bf),
            jax.ShapeDtypeStruct((count, width), bf),
            jax.ShapeDtypeStruct((count, 128), jnp.float32),
        ),
        in_specs=[vmem] * 2,
        out_specs=(vmem, vmem, vmem),
        scratch_shapes=[
            pltpu.VMEM((ncol, nblk, rows, cols, width), bf),
            edges,
            edges,
            (
                pltpu.VMEM((1, cols, 128), jnp.float32),
                pltpu.VMEM((1, cols, 128), jnp.float32),
                pltpu.VMEM((rows, SIDE, 128), jnp.float32),
                pltpu.VMEM((rows, SIDE, 128), jnp.float32),
            ),
            pltpu.VMEM((rows, cols, width), bf),
            pltpu.VMEM((rows, cols, 128), jnp.float32),
            pltpu.VMEM((rows * cols, width), bf),
            pltpu.VMEM((rows + 4, cols + SIDE, width), jnp.float32),
            pltpu.VMEM((rows + 4, cols + SIDE, 128), jnp.float32),
            pltpu.VMEM((rows * cols, 128), jnp.float32),
            pltpu.VMEM((rows * cols, width), jnp.float32),
            pltpu.VMEM((rows * cols, 128), jnp.float32),
            dma((ncol, nblk, 2)),
            dma((nz - 1, 2)),
            dma((2, ncol, nz)),
            dma((2, ncol - 1, nz, 2)),
            dma((ncol, nblk // 2, 2)),
            dma((20,)),
            dma((20,)),
        ],
        compiler_params=pltpu.CompilerParams(
            collective_id=0, has_side_effects=True, vmem_limit_bytes=48 * 1024 * 1024
        ),
    )(feat1, feat2)
    return pl.pallas_call(
        functools.partial(stencil, nblk, ncol, rows, cols),
        out_shape=(
            jax.ShapeDtypeStruct((2, rows, cols), jnp.float32),
            jax.ShapeDtypeStruct((2, rows, cols), jnp.float32),
            jax.ShapeDtypeStruct((rows, cols, width), jnp.float32),
        ),
        in_specs=[vmem] * 3,
        out_specs=(vmem, vmem, vmem),
        compiler_params=pltpu.CompilerParams(vmem_limit_bytes=40 * 1024 * 1024),
    )(xq, warped, sums)


def solution(mesh):
    placed = (P("blk", "col", None), P("blk", "col", None))
    return jax.shard_map(
        functools.partial(body, mesh.shape["blk"], mesh.shape["col"]),
        mesh=mesh,
        in_specs=placed,
        out_specs=(P(None, "blk", "col"), P(None, "blk", "col"), P("blk", "col", None)),
        check_vma=False,
    )
```
